512 devices in a mesh: gx: 16 (over y, core), gy: 32 (over x, z).
Axes of the slice: x: 4, y: 8, z: 8, core: 2. Of those that a mesh axis runs over, the one named last changes fastest.
Arguments:
- head_before: float32 [8, 256, 32768], P(None, 'gx', 'gy'), may hold values from -6 to 6
- log_conductivity: float32 [256, 32768], P('gx', 'gy'), may hold values from -2.5 to 2.5
- fixed_mask: int32 [256, 32768], P('gx', 'gy'), may hold values 0 or 1
- well_cells: int32 [8], replicated, may hold values from 0 to 8388607
- pump_rates: float32 [8], replicated, may hold values from 50 to 500
- adjoint_seed: float32 [8, 256, 32768], P(None, 'gx', 'gy'), may hold values from -6 to 6
Outputs:
- heads: float32 [8, 256, 32768], P(None, 'gx', 'gy')
- conductivity_sensitivity: float32 [256, 32768], P('gx', 'gy')
The draws below stay inside these ranges and needn't reach their ends.
All inputs are finite; a program needn't handle non-finite values. No bound on the sum of `fixed_mask` on one device may be relied on, other than what follows from the above.
Results may differ from the reference program's by a relative error of at most 0.00045.
Values sent between devices are 32-bit elements; how exact they have to be, the bound alone decides.
No kernel may reach another device: no remote copies, remote signals or barrier semaphores. Data moves between devices by JAX's collectives and lax.ppermute only.
A program may use at most 64 MiB of HBM per device.

```python
import math
import jax
import jax.numpy as jnp
from jax import lax

TESTS = 8
NX = 256
NY = 32768


def draw_log_conductivity(key, part):
    values = jnp.clip(0.5 * jax.random.normal(key, (NX, NY), jnp.float32), -2.5, 2.5)
    return values


def place_ends(drawn, stream_key, low, high):
    extent = drawn.shape
    place = [jax.random.randint(jax.random.fold_in(stream_key, axis), (), 0, extent[axis]) for axis in range(len(extent))]
    drawn = drawn.at[tuple(place)].set(low)
    longest = extent.index(max(extent))
    place[longest] = (place[longest] + 1) % extent[longest]
    return drawn.at[tuple(place)].set(high)


def level_of(rng, extent, pieces, least, top_value):
    factor_of, own = 1.0, jax.random.fold_in(rng, 6)
    for position, shards_of in pieces:
        heights = jnp.exp(jax.random.uniform(jax.random.fold_in(own, position), (shards_of,), jnp.float32, least / len(pieces), top_value / len(pieces)))
        factor_of = factor_of * jnp.repeat(heights, extent[position] // shards_of).reshape([-1 if axis == position else 1 for axis in range(len(extent))])
    return factor_of


def scatter_about(rng, extent, scale, bound, split=(), held_as=jnp.bfloat16):
    array = jax.random.normal(rng, extent, jnp.float32) * scale
    if len(split) > 0:
        array = level_of(rng, extent, split, -0.22, 0.18) * array
    return jnp.clip(array, min=-bound, max=bound).astype(held_as)


def setup_inputs(seed: int = 0) -> dict:
    seeds = jax.random.split(jax.random.key(seed), 7)
    return {
        "head_before": scatter_about(seeds[0], (TESTS, NX, NY), 1.0, 6.0, ((1, 16), (2, 32)), jnp.float32),
        "log_conductivity": draw_log_conductivity(jax.random.fold_in(seeds[6], 71), 0),
        "fixed_mask": place_ends((jax.random.randint(seeds[2], (NX, NY), 0, 1024) < 1).astype(jnp.int32), jax.random.fold_in(seeds[2], 1), 0, 1),
        "well_cells": place_ends(jax.random.randint(seeds[3], (TESTS,), 0, NX * NY), jax.random.fold_in(seeds[3], 1), 0, (NX * NY) - 1).astype(jnp.int32),
        "pump_rates": jnp.clip(jnp.exp(jax.random.uniform(seeds[4], (TESTS,), jnp.float32, math.log(50.0), math.log(500.0))), 50.0, 500.0),
        "adjoint_seed": scatter_about(seeds[5], (TESTS, NX, NY), 1.0, 6.0, ((1, 16), (2, 32)), jnp.float32),
    }


implicit_ratio = 4000.0
explicit_ratio = 0.1


def harmonic(own_value, other_value):
    return 2.0 * own_value * other_value / (own_value + other_value)


def face_slope(own_value, other_value):
    summed = own_value + other_value
    return 2.0 * own_value * other_value * other_value / (summed * summed)


def thomas(lower, middle, upper, right_side):
    column_count = middle.shape[1]
    test_count = right_side.shape[0]

    def forward_step(state_pair, inputs):
        prior_upper, prior_rhs = state_pair
        row_lower, row_middle, row_upper, row_rhs = inputs
        pivot = row_middle - row_lower * prior_upper
        new_upper = row_upper / pivot
        new_rhs = (row_rhs - row_lower * prior_rhs) / pivot
        return (new_upper, new_rhs), (new_upper, new_rhs)

    initial = (jnp.zeros((column_count,), jnp.float32), jnp.zeros((test_count, column_count), jnp.float32))
    _, (uppers, rights) = lax.scan(forward_step, initial, (lower, middle, upper, jnp.moveaxis(right_side, 1, 0)))

    def back_step(later_value, inputs):
        row_upper, row_rhs = inputs
        value = row_rhs - row_upper * later_value
        return value, value

    _, values = lax.scan(back_step, jnp.zeros((test_count, column_count), jnp.float32), (uppers, rights), reverse=True)
    return jnp.moveaxis(values, 0, 1)


def reference(head_before, log_conductivity, fixed_mask, well_cells, pump_rates, adjoint_seed):
    test_count, row_count, column_count = head_before.shape
    active = (1 - fixed_mask).astype(jnp.float32)
    conduct = jnp.exp(log_conductivity)
    cond_pad = jnp.pad(conduct, 1)
    act_pad = jnp.pad(active, 1)
    west_cond = cond_pad[:-2, 1:-1]
    east_cond = cond_pad[2:, 1:-1]
    south_cond = cond_pad[1:-1, :-2]
    north_cond = cond_pad[1:-1, 2:]
    west_act = act_pad[:-2, 1:-1]
    east_act = act_pad[2:, 1:-1]
    south_act = act_pad[1:-1, :-2]
    north_act = act_pad[1:-1, 2:]
    west_face = harmonic(conduct, west_cond)
    east_face = harmonic(conduct, east_cond)
    south_face = harmonic(conduct, south_cond)
    north_face = harmonic(conduct, north_cond)
    head_pad = jnp.pad(head_before, ((0, 0), (0, 0), (1, 1)))
    spread = north_face * (head_pad[:, :, 2:] - head_before) + south_face * (head_pad[:, :, :-2] - head_before)
    cell_number = jnp.arange(row_count * column_count, dtype=jnp.int32).reshape(row_count, column_count)
    well_here = cell_number[None] == well_cells[:, None, None]
    source = jnp.where(well_here, pump_rates[:, None, None], jnp.zeros((), jnp.float32))
    right_side = head_before + active * (explicit_ratio * spread + source)
    lower = -implicit_ratio * west_face * active
    upper = -implicit_ratio * east_face * active
    middle = 1.0 + implicit_ratio * (west_face + east_face) * active
    heads = thomas(lower, middle, upper, right_side)
    adjoint_field = thomas(-implicit_ratio * west_face * west_act, middle, -implicit_ratio * east_face * east_act, adjoint_seed)
    heads_pad = jnp.pad(heads, ((0, 0), (1, 1), (0, 0)))
    adj_rows = jnp.pad(adjoint_field, ((0, 0), (1, 1), (0, 0)))
    adj_cols = jnp.pad(adjoint_field, ((0, 0), (0, 0), (1, 1)))
    own_weight = adjoint_field * active
    west_term = jnp.sum((heads_pad[:, :-2] - heads) * (own_weight - adj_rows[:, :-2] * west_act), axis=0)
    east_term = jnp.sum((heads_pad[:, 2:] - heads) * (own_weight - adj_rows[:, 2:] * east_act), axis=0)
    south_term = jnp.sum((head_pad[:, :, :-2] - head_before) * (own_weight - adj_cols[:, :, :-2] * south_act), axis=0)
    north_term = jnp.sum((head_pad[:, :, 2:] - head_before) * (own_weight - adj_cols[:, :, 2:] * north_act), axis=0)
    sensitivity = implicit_ratio * (west_term * face_slope(conduct, west_cond) + east_term * face_slope(conduct, east_cond))
    sensitivity = sensitivity + explicit_ratio * (south_term * face_slope(conduct, south_cond) + north_term * face_slope(conduct, north_cond))
    return heads, sensitivity
```

```python
import functools

import jax
import jax.numpy as jnp
from jax import lax
from jax.experimental import pallas as pl
from jax.experimental.pallas import tpu as pltpu
from jax.sharding import PartitionSpec as P

implicit_ratio = 4000.0
explicit_ratio = 0.1
LANES = 128
SUBLANES = 8


def spread_columns(lane, pieces):
    out = jnp.zeros(lane.shape, jnp.float32)
    for low, count, column in pieces:
        out = jnp.where((lane >= low) & (lane < low + count), column, out)
    return out


def edge_kernel(rows, tests, hb0, hb1, seed0, seed1, logk0, logk1, mask0, mask1, to_right, to_left, own):
    lane = lax.broadcasted_iota(jnp.int32, (rows, LANES), 1)
    sides = []
    for hb, seed, logk, mask, c in ((hb0, seed0, logk0, mask0, 0), (hb1, seed1, logk1, mask1, LANES - 1)):
        conduct = jnp.exp(logk[:, c : c + 1])
        active = (1 - mask[:, c : c + 1]).astype(jnp.float32)
        heads = [hb[rows * t : rows * (t + 1), c : c + 1] for t in range(tests)]
        seeds = [active * seed[rows * t : rows * (t + 1), c : c + 1] for t in range(tests)]
        sides.append((conduct, active, heads, seeds))

    def packed(side, odd, with_seed):
        conduct, active, heads, seeds = sides[side]
        base = tests * odd
        pieces = [(2 * tests + base + t, 1, heads[t]) for t in range(tests)]
        pieces += [(4 * tests + base, tests, conduct), (6 * tests + base, tests, active)]
        if with_seed:
            pieces += [(base + t, 1, seeds[t]) for t in range(tests)]
        return spread_columns(lane, pieces)

    to_right[...] = packed(1, 0, True)
    to_left[...] = packed(0, 1, True)
    own[...] = packed(0, 0, False) + packed(1, 1, False)


def eliminate(conduct, active):
    rows = len(conduct)
    gains, inverses, backs = [None], [], []
    excess = jnp.ones_like(conduct[0])
    face = None
    for i in range(rows):
        if i > 0:
            gain = active[i] * face * inverses[-1]
            gains.append(gain)
            excess = 1.0 + gain * excess
        if i < rows - 1:
            face = (2.0 * implicit_ratio) * conduct[i] * conduct[i + 1] / (conduct[i] + conduct[i + 1])
            upper = active[i] * face
            inverse = 1.0 / (excess + upper)
            backs.append(upper * inverse)
        else:
            inverse = 1.0 / excess
            backs.append(None)
        inverses.append(inverse)
    return gains, inverses, backs


def sweep(gains, inverses, backs, right):
    rows = len(right)
    held = [right[0]]
    for i in range(1, rows):
        held.append(right[i] + gains[i] * held[-1])
    values = [None] * rows
    values[-1] = held[-1] * inverses[-1]
    for i in range(rows - 2, -1, -1):
        values[i] = held[i] * inverses[i] + backs[i] * values[i + 1]
    return values


def responses(gains, inverses, backs, active):
    rows = len(active)
    held = [active[0]]
    for i in range(1, rows):
        held.append(gains[i] * held[-1])
    first, last = [None] * rows, [None] * rows
    first[-1] = held[-1] * inverses[-1]
    last[-1] = active[-1] * inverses[-1]
    for i in range(rows - 2, -1, -1):
        first[i] = held[i] * inverses[i] + backs[i] * first[i + 1]
        last[i] = backs[i] * last[i + 1]
    return first, last


def local_kernel(
    rows, tests, total_columns, wells, rates, hb, seed, logk, mask, from_left, from_right, own,
    message, heads_part, adjoint_part, first_out, last_out, side_part, side_first, side_last,
    right, weighed, cond_c, act_c, gain_c, inv_c, back_c, first_c, last_c,
):
    columns = hb.shape[1]
    tiles = columns // LANES
    field = tests * rows
    conduct = jnp.exp(logk[...])
    active = (1 - mask[...]).astype(jnp.float32)
    for k in range(tiles):
        cond_c[pl.ds(k, rows, stride=tiles), :] = conduct[:, k * LANES : (k + 1) * LANES]
        act_c[pl.ds(k, rows, stride=tiles), :] = active[:, k * LANES : (k + 1) * LANES]
    cond_rows = [cond_c[tiles * i : tiles * (i + 1), :] for i in range(rows)]
    act_rows = [act_c[tiles * i : tiles * (i + 1), :] for i in range(rows)]
    gains, inverses, backs = eliminate(cond_rows, act_rows)
    first, last = responses(gains, inverses, backs, act_rows)
    for i in range(rows):
        here = slice(tiles * i, tiles * (i + 1))
        if i > 0:
            gain_c[here, :] = gains[i]
        inv_c[here, :] = inverses[i]
        if i < rows - 1:
            back_c[here, :] = backs[i]
        first_c[here, :] = first[i]
        last_c[here, :] = last[i]
    half = 0.5 / implicit_ratio
    first_end = first[0] + half / cond_rows[0]
    last_end = last[-1] + half / cond_rows[-1]
    across = first[-1]

    lane = lax.broadcasted_iota(jnp.int32, (rows, columns), 1)
    cond_north = pltpu.roll(conduct, columns - 1, 1)
    face = (2.0 * explicit_ratio) * conduct * cond_north / (conduct + cond_north)
    face = jnp.where(lane == columns - 1, 0.0, face)
    for t in range(tests):
        here = slice(rows * t, rows * (t + 1))
        head = hb[here, :]
        flow = face * (pltpu.roll(head, columns - 1, 1) - head)
        value = head + active * (flow - pltpu.roll(flow, 1, 1))
        seeded = active * seed[here, :]
        for k in range(tiles):
            lanes = slice(k * LANES, (k + 1) * LANES)
            there = slice(k * field + rows * t, k * field + rows * (t + 1))
            right[there, :] = value[:, lanes]
            weighed[there, :] = seeded[:, lanes]
    row_start = lax.axis_index("gx") * rows
    column_start = lax.axis_index("gy") * columns
    row_lane = lax.broadcasted_iota(jnp.int32, (1, LANES), 1)
    for t in range(tests):
        well = wells[t]
        well_row = well // total_columns - row_start
        well_column = well % total_columns - column_start
        inside = (well_row >= 0) & (well_row < rows) & (well_column >= 0) & (well_column < columns)

        @pl.when(inside)
        def _():
            tile = well_column // LANES
            act_row = act_c[pl.ds(tiles * well_row + tile, 1), :]
            there = pl.ds(tile * field + rows * t + well_row, 1)
            added = jnp.where(row_lane == well_column % LANES, act_row * rates[t], 0.0)
            right[there, :] = right[there, :] + added

    for k in range(tiles):
        lanes = slice(k * LANES, (k + 1) * LANES)
        gain_k = [None] + [gain_c[tiles * i + k : tiles * i + k + 1, :] for i in range(1, rows)]
        inv_k = [inv_c[tiles * i + k : tiles * i + k + 1, :] for i in range(rows)]
        back_k = [back_c[tiles * i + k : tiles * i + k + 1, :] for i in range(rows - 1)] + [None]
        for core, (source, out) in enumerate(((right, heads_part), (weighed, adjoint_part))):
            given = [source[pl.ds(k * field + i, tests, stride=rows), :] for i in range(rows)]
            values = sweep(gain_k, inv_k, back_k, given)
            for i in range(rows):
                out[pl.ds(k * field + i, tests, stride=rows), :] = values[i]
            dest = 2 * k + core
            message[dest, 0:tests, :] = values[0]
            message[dest, tests : 2 * tests, :] = values[-1]
            message[dest, 16:17, :] = first_end[k : k + 1, :]
            message[dest, 17:18, :] = last_end[k : k + 1, :]
            message[dest, 18:19, :] = across[k : k + 1, :]
        first_out[:, lanes] = first_c[pl.ds(k, rows, stride=tiles), :]
        last_out[:, lanes] = last_c[pl.ds(k, rows, stride=tiles), :]

    halo = from_left[...] + from_right[...]
    mine = own[...]
    side_lane = lax.broadcasted_iota(jnp.int32, (rows, LANES), 1)
    outer = side_lane < 2 * tests
    halo_k = pltpu.roll(halo, LANES - 2 * tests, 1)
    own_k = pltpu.roll(mine, LANES - 2 * tests, 1)
    cond_s = jnp.where(outer, pltpu.roll(halo, LANES - 4 * tests, 1), own_k)
    cond_s = jnp.where(cond_s > 0.0, cond_s, 1.0)
    act_s = jnp.where(outer, pltpu.roll(halo, LANES - 6 * tests, 1), pltpu.roll(mine, LANES - 4 * tests, 1))
    side_face = (2.0 * explicit_ratio) * cond_s * halo_k / (cond_s + halo_k)
    given_s = jnp.where(outer, halo, act_s * side_face * (halo - mine))
    cond_sr = [cond_s[i : i + 1, :] for i in range(rows)]
    act_sr = [act_s[i : i + 1, :] for i in range(rows)]
    gains_s, inv_s, backs_s = eliminate(cond_sr, act_sr)
    first_s, last_s = responses(gains_s, inv_s, backs_s, act_sr)
    part_s = sweep(gains_s, inv_s, backs_s, [given_s[i : i + 1, :] for i in range(rows)])
    for i in range(rows):
        side_part[i : i + 1, :] = part_s[i]
        side_first[i : i + 1, :] = first_s[i]
        side_last[i : i + 1, :] = last_s[i]
    ends = (
        part_s[0], part_s[-1], first_s[0] + half / cond_sr[0], last_s[-1] + half / cond_sr[-1], first_s[-1],
    )
    for dest in range(2 * tiles):
        for r, value in enumerate(ends):
            message[dest, 19 + r : 20 + r, :] = value


def chain(first_end, last_end, across, first_value, last_value):
    count = len(first_end)
    diag = [None] + [last_end[i - 1] + first_end[i] for i in range(1, count)]
    load = [None] + [last_value[i - 1] - first_value[i] for i in range(1, count)]
    middle = count // 2
    inverse = [None] * count
    for i in range(1, middle):
        if i > 1:
            factor = across[i - 1] * inverse[i - 1]
            diag[i] = diag[i] - factor * across[i - 1]
            load[i] = load[i] + factor * load[i - 1]
        inverse[i] = 1.0 / diag[i]
    for i in range(count - 1, middle, -1):
        if i < count - 1:
            factor = across[i] * inverse[i + 1]
            diag[i] = diag[i] - factor * across[i]
            load[i] = load[i] + factor * load[i + 1]
        inverse[i] = 1.0 / diag[i]
    below = across[middle - 1] * inverse[middle - 1]
    above = across[middle] * inverse[middle + 1]
    diag[middle] = diag[middle] - below * across[middle - 1] - above * across[middle]
    load[middle] = load[middle] + below * load[middle - 1] + above * load[middle + 1]
    flux = [None] * count
    flux[middle] = load[middle] / diag[middle]
    for i in range(middle - 1, 0, -1):
        flux[i] = (load[i] + across[i] * flux[i + 1]) * inverse[i]
    for i in range(middle + 1, count):
        flux[i] = (load[i] + across[i - 1] * flux[i - 1]) * inverse[i]
    nothing = jnp.zeros_like(flux[middle])
    return [nothing] + flux[1:] + [nothing]


def line_kernel(devices, tests, got, reply, side_flux, held):
    def solve(first_end, last_end, across, first_value, last_value):
        def pick(span):
            return [got[d, span, :] for d in range(devices)]

        return chain(pick(first_end), pick(last_end), pick(across), pick(first_value), pick(last_value))

    side = solve(slice(21, 22), slice(22, 23), slice(23, 24), slice(19, 20), slice(20, 21))
    for d in range(devices + 1):
        held[d : d + 1, :] = side[d]
    flux = solve(slice(16, 17), slice(17, 18), slice(18, 19), slice(0, tests), slice(tests, 2 * tests))
    for d in range(devices):
        reply[d, 0:tests, :] = flux[d]
        reply[d, tests : 2 * tests, :] = flux[d + 1]
    me = lax.axis_index("gx")
    side_flux[0:1, :] = held[pl.ds(me, 1), :]
    side_flux[1:2, :] = held[pl.ds(me + 1, 1), :]


def final_kernel(
    rows, tests, hb, logk, heads_part, adjoint_part, first_in, last_in, got, from_left, from_right,
    side_part, side_first, side_last, side_flux, heads, sensitivity,
):
    columns = hb.shape[1]
    tiles = columns // LANES
    side = side_part[...] + side_first[...] * side_flux[0:1, :] - side_last[...] * side_flux[1:2, :]
    halo = from_left[...] + from_right[...]
    conduct = jnp.exp(logk[...])
    first = first_in[...]
    last = last_in[...]
    lane = lax.broadcasted_iota(jnp.int32, (rows, columns), 1)
    row = lax.broadcasted_iota(jnp.int32, (rows, columns), 0)
    at_start = lane == 0
    at_end = lane == columns - 1

    def wide(core, r):
        return jnp.concatenate([got[2 * k + core, r : r + 1, :] for k in range(tiles)], axis=1)

    def joined(part, t):
        starts = [(k * tests + t) * rows for k in range(tiles)]
        return jnp.concatenate([part[start : start + rows, :] for start in starts], axis=1)

    def beside(values, index):
        return values[:, index : index + 1]

    row_lane = lax.broadcasted_iota(jnp.int32, (1, columns), 1)
    end_products = [jnp.zeros((1, columns), jnp.float32)] * 2
    along_rows = jnp.zeros((rows, columns), jnp.float32)
    along_columns = jnp.zeros((rows, columns), jnp.float32)
    start_face = jnp.zeros((rows, LANES), jnp.float32)
    for t in range(tests):
        here = slice(rows * t, rows * (t + 1))
        fluxes = [[wide(core, base + t) for base in (0, tests)] for core in (0, 1)]
        head = joined(heads_part, t) + first * fluxes[0][0] - last * fluxes[0][1]
        head = head + jnp.where(at_start, beside(side, 2 * tests + t), 0.0)
        head = head + jnp.where(at_end, beside(side, 3 * tests + t), 0.0)
        heads[here, :] = head
        weight = joined(adjoint_part, t) + first * fluxes[1][0] - last * fluxes[1][1]
        for end in (0, 1):
            side_row = side_flux[end : end + 1, :]
            whole = fluxes[0][end] + jnp.where(row_lane == 0, beside(side_row, 2 * tests + t), 0.0)
            whole = whole + jnp.where(row_lane == columns - 1, beside(side_row, 3 * tests + t), 0.0)
            end_products[end] = end_products[end] + whole * fluxes[1][end]
        east_head = pltpu.roll(head, rows - 1, 0)
        east_weight = pltpu.roll(weight, rows - 1, 0)
        along_rows = along_rows + (east_head - head) * (weight - east_weight)
        old = hb[here, :]
        north_old = jnp.where(at_end, beside(halo, 3 * tests + t), pltpu.roll(old, columns - 1, 1))
        north_weight = jnp.where(at_end, beside(side, tests + t), pltpu.roll(weight, columns - 1, 1))
        along_columns = along_columns + (north_old - old) * (weight - north_weight)
        start_face = start_face + (old[:, :LANES] - beside(halo, 2 * tests + t)) * (
            beside(side, t) - weight[:, :LANES]
        )
    cond_east = pltpu.roll(conduct, rows - 1, 0)
    face = 2.0 * conduct * cond_east / (conduct + cond_east)
    face = jnp.where(row == rows - 1, 0.0, face)
    share = implicit_ratio * face * face * along_rows
    total = share + pltpu.roll(share, 1, 0)
    cond_north = jnp.where(at_end, beside(halo, 5 * tests), pltpu.roll(conduct, columns - 1, 1))
    face = 2.0 * conduct * cond_north / (conduct + cond_north)
    share = explicit_ratio * face * face * along_columns
    cond_start = conduct[:, :LANES]
    cond_south = jnp.broadcast_to(beside(halo, 4 * tests), (rows, LANES))
    face = 2.0 * cond_start * cond_south / (cond_start + cond_south)
    start_share = explicit_ratio * face * face * start_face
    start_share = jnp.concatenate([start_share, jnp.zeros((rows, columns - LANES), jnp.float32)], axis=1)
    total = total + share + jnp.where(at_start, start_share, pltpu.roll(share, 1, 1))
    scale = -1.0 / implicit_ratio
    total = total + jnp.where(row == 0, scale * end_products[0], 0.0)
    total = total + jnp.where(row == rows - 1, scale * end_products[1], 0.0)
    sensitivity[...] = total * (0.5 / conduct)


def f32(*shape):
    return jax.ShapeDtypeStruct(shape, jnp.float32)


VMEM = pl.BlockSpec(memory_space=pltpu.VMEM)
SMEM = pl.BlockSpec(memory_space=pltpu.SMEM)
PARAMS = pltpu.CompilerParams(vmem_limit_bytes=40 * 1024 * 1024)


def per_device(head_before, log_conductivity, fixed_mask, well_cells, pump_rates, adjoint_seed):
    tests, rows, columns = head_before.shape
    tiles = columns // LANES
    devices = lax.axis_size("gx")
    peers = lax.axis_size("gy")
    hb = head_before.reshape(tests * rows, columns)
    seed = adjoint_seed.reshape(tests * rows, columns)

    def ends(height):
        return [pl.BlockSpec((height, LANES), lambda i, k=k: (0, k)) for k in (0, tiles - 1)]

    small = pl.BlockSpec((rows, LANES), lambda i: (0, 0))
    to_right, to_left, own = pl.pallas_call(
        functools.partial(edge_kernel, rows, tests),
        grid=(1,),
        in_specs=ends(tests * rows) * 2 + ends(rows) * 2,
        out_specs=[small] * 3,
        out_shape=[f32(rows, LANES)] * 3,
        compiler_params=PARAMS,
        name="edges",
    )(hb, hb, seed, seed, log_conductivity, log_conductivity, fixed_mask, fixed_mask)
    from_left = lax.ppermute(to_right, "gy", [(i, i + 1) for i in range(peers - 1)])
    from_right = lax.ppermute(to_left, "gy", [(i + 1, i) for i in range(peers - 1)])

    part = f32(tiles * tests * rows, LANES)
    message, heads_part, adjoint_part, first, last, side_part, side_first, side_last = pl.pallas_call(
        functools.partial(local_kernel, rows, tests, columns * peers),
        in_specs=[SMEM] * 2 + [VMEM] * 7,
        out_specs=[VMEM] * 8,
        out_shape=[f32(devices, 24, LANES), part, part] + [f32(rows, columns)] * 2 + [f32(rows, LANES)] * 3,
        scratch_shapes=[pltpu.VMEM((tiles * tests * rows, LANES), jnp.float32)] * 2
        + [pltpu.VMEM((rows * tiles, LANES), jnp.float32)] * 7,
        compiler_params=PARAMS,
        name="local",
    )(well_cells, pump_rates, hb, seed, log_conductivity, fixed_mask, from_left, from_right, own)
    got = lax.all_to_all(message, "gx", 0, 0)
    reply, side_flux = pl.pallas_call(
        functools.partial(line_kernel, devices, tests),
        in_specs=[VMEM],
        out_specs=[VMEM] * 2,
        out_shape=[f32(devices, 2 * tests, LANES), f32(SUBLANES, LANES)],
        scratch_shapes=[pltpu.VMEM((devices + SUBLANES, LANES), jnp.float32)],
        compiler_params=PARAMS,
        name="line",
    )(got)
    answer = lax.all_to_all(reply, "gx", 0, 0)
    heads, sensitivity = pl.pallas_call(
        functools.partial(final_kernel, rows, tests),
        in_specs=[VMEM] * 13,
        out_specs=[VMEM] * 2,
        out_shape=[f32(tests * rows, columns), f32(rows, columns)],
        compiler_params=PARAMS,
        name="final",
    )(
        hb, log_conductivity, heads_part, adjoint_part, first, last, answer, from_left, from_right,
        side_part, side_first, side_last, side_flux,
    )
    return heads.reshape(tests, rows, columns), sensitivity


def solution(mesh):
    return jax.shard_map(
        per_device,
        mesh=mesh,
        in_specs=(P(None, "gx", "gy"), P("gx", "gy"), P("gx", "gy"), P(), P(), P(None, "gx", "gy")),
        out_specs=(P(None, "gx", "gy"), P("gx", "gy")),
        check_vma=False,
    )
```

```python
import functools

import jax
import jax.numpy as jnp
from jax import lax
from jax.experimental import pallas as pl
from jax.experimental.pallas import tpu as pltpu
from jax.sharding import PartitionSpec as P

implicit_ratio = 4000.0
explicit_ratio = 0.1
LANES = 128
SUBLANES = 8


def spread_columns(lane, pieces):
    out = jnp.zeros(lane.shape, jnp.float32)
    for low, count, column in pieces:
        out = jnp.where((lane >= low) & (lane < low + count), column, out)
    return out


def edge_messages(rows, tests, hb, seed, conduct, active, to_right, to_left, own):
    columns = hb.shape[1]
    lane = lax.broadcasted_iota(jnp.int32, (rows, LANES), 1)
    sides = []
    for c in (0, columns - 1):
        column = slice(c, c + 1)
        heads = [hb[rows * t : rows * (t + 1), column] for t in range(tests)]
        seeds = [active[:, column] * seed[rows * t : rows * (t + 1), column] for t in range(tests)]
        sides.append((conduct[:, column], active[:, column], heads, seeds))

    def packed(side, odd, with_seed):
        conduct, active, heads, seeds = sides[side]
        base = tests * odd
        pieces = [(2 * tests + base + t, 1, heads[t]) for t in range(tests)]
        pieces += [(4 * tests + base, tests, conduct), (6 * tests + base, tests, active)]
        if with_seed:
            pieces += [(base + t, 1, seeds[t]) for t in range(tests)]
        return spread_columns(lane, pieces)

    to_right[...] = packed(1, 0, True)
    to_left[...] = packed(0, 1, True)
    own[...] = packed(0, 0, False) + packed(1, 1, False)


def eliminate(conduct, active):
    rows = len(conduct)
    gains, inverses, backs = [None], [], []
    excess = jnp.ones_like(conduct[0])
    face = None
    for i in range(rows):
        if i > 0:
            gain = active[i] * face * inverses[-1]
            gains.append(gain)
            excess = 1.0 + gain * excess
        if i < rows - 1:
            face = (2.0 * implicit_ratio) * conduct[i] * conduct[i + 1] / (conduct[i] + conduct[i + 1])
            upper = active[i] * face
            inverse = 1.0 / (excess + upper)
            backs.append(upper * inverse)
        else:
            inverse = 1.0 / excess
            backs.append(None)
        inverses.append(inverse)
    return gains, inverses, backs


def sweep(gains, inverses, backs, right):
    rows = len(right)
    held = [right[0]]
    for i in range(1, rows):
        held.append(right[i] + gains[i] * held[-1])
    values = [None] * rows
    values[-1] = held[-1] * inverses[-1]
    for i in range(rows - 2, -1, -1):
        values[i] = held[i] * inverses[i] + backs[i] * values[i + 1]
    return values


def responses(gains, inverses, backs, active):
    rows = len(active)
    held = [active[0]]
    for i in range(1, rows):
        held.append(gains[i] * held[-1])
    first, last = [None] * rows, [None] * rows
    first[-1] = held[-1] * inverses[-1]
    last[-1] = active[-1] * inverses[-1]
    for i in range(rows - 2, -1, -1):
        first[i] = held[i] * inverses[i] + backs[i] * first[i + 1]
        last[i] = backs[i] * last[i + 1]
    return first, last


def local_kernel(
    rows, tests, total_columns, wells, rates, hb_all, seed_all, logk_all, mask_all,
    message, heads_part, adjoint_part, first_out, last_out, to_right, to_left, own,
    hb, seed, logk, mask, arrived, right, weighed, cond_c, act_c, gain_c, inv_c, back_c, first_c, last_c,
):
    copies = [
        pltpu.make_async_copy(whole, here, arrived.at[n])
        for n, (whole, here) in enumerate(((logk_all, logk), (mask_all, mask), (hb_all, hb), (seed_all, seed)))
    ]
    for copy in copies:
        copy.start()
    columns = hb.shape[1]
    tiles = columns // LANES
    field = tests * rows
    copies[0].wait()
    copies[1].wait()
    conduct = jnp.exp(logk[...])
    active = (1 - mask[...]).astype(jnp.float32)
    for k in range(tiles):
        cond_c[pl.ds(k, rows, stride=tiles), :] = conduct[:, k * LANES : (k + 1) * LANES]
        act_c[pl.ds(k, rows, stride=tiles), :] = active[:, k * LANES : (k + 1) * LANES]
    cond_rows = [cond_c[tiles * i : tiles * (i + 1), :] for i in range(rows)]
    act_rows = [act_c[tiles * i : tiles * (i + 1), :] for i in range(rows)]
    gains, inverses, backs = eliminate(cond_rows, act_rows)
    first, last = responses(gains, inverses, backs, act_rows)
    for i in range(rows):
        here = slice(tiles * i, tiles * (i + 1))
        if i > 0:
            gain_c[here, :] = gains[i]
        inv_c[here, :] = inverses[i]
        if i < rows - 1:
            back_c[here, :] = backs[i]
        first_c[here, :] = first[i]
        last_c[here, :] = last[i]
    half = 0.5 / implicit_ratio
    first_end = first[0] + half / cond_rows[0]
    last_end = last[-1] + half / cond_rows[-1]
    across = first[-1]

    copies[2].wait()
    copies[3].wait()
    edge_messages(rows, tests, hb, seed, conduct, active, to_right, to_left, own)

    lane = lax.broadcasted_iota(jnp.int32, (rows, columns), 1)
    cond_north = pltpu.roll(conduct, columns - 1, 1)
    face = (2.0 * explicit_ratio) * conduct * cond_north / (conduct + cond_north)
    face = jnp.where(lane == columns - 1, 0.0, face)
    for t in range(tests):
        here = slice(rows * t, rows * (t + 1))
        head = hb[here, :]
        flow = face * (pltpu.roll(head, columns - 1, 1) - head)
        value = head + active * (flow - pltpu.roll(flow, 1, 1))
        seeded = active * seed[here, :]
        for k in range(tiles):
            lanes = slice(k * LANES, (k + 1) * LANES)
            there = slice(k * field + rows * t, k * field + rows * (t + 1))
            right[there, :] = value[:, lanes]
            weighed[there, :] = seeded[:, lanes]
    row_start = lax.axis_index("gx") * rows
    column_start = lax.axis_index("gy") * columns
    row_lane = lax.broadcasted_iota(jnp.int32, (1, LANES), 1)
    for t in range(tests):
        well = wells[t]
        well_row = well // total_columns - row_start
        well_column = well % total_columns - column_start
        inside = (well_row >= 0) & (well_row < rows) & (well_column >= 0) & (well_column < columns)

        @pl.when(inside)
        def _():
            tile = well_column // LANES
            act_row = act_c[pl.ds(tiles * well_row + tile, 1), :]
            there = pl.ds(tile * field + rows * t + well_row, 1)
            added = jnp.where(row_lane == well_column % LANES, act_row * rates[t], 0.0)
            right[there, :] = right[there, :] + added

    for k in range(tiles):
        lanes = slice(k * LANES, (k + 1) * LANES)
        gain_k = [None] + [gain_c[tiles * i + k : tiles * i + k + 1, :] for i in range(1, rows)]
        inv_k = [inv_c[tiles * i + k : tiles * i + k + 1, :] for i in range(rows)]
        back_k = [back_c[tiles * i + k : tiles * i + k + 1, :] for i in range(rows - 1)] + [None]
        for core, (source, out) in enumerate(((right, heads_part), (weighed, adjoint_part))):
            given = [source[pl.ds(k * field + i, tests, stride=rows), :] for i in range(rows)]
            values = sweep(gain_k, inv_k, back_k, given)
            for i in range(rows):
                start = k * field + i * tests
                out[start : start + tests, :] = values[i]
            dest = 2 * k + core
            message[dest, 0:tests, :] = values[0]
            message[dest, tests : 2 * tests, :] = values[-1]
            message[dest, 16:17, :] = first_end[k : k + 1, :]
            message[dest, 17:18, :] = last_end[k : k + 1, :]
            message[dest, 18:19, :] = across[k : k + 1, :]
        first_out[:, lanes] = first_c[pl.ds(k, rows, stride=tiles), :]
        last_out[:, lanes] = last_c[pl.ds(k, rows, stride=tiles), :]


def chain(first_end, last_end, across, first_value, last_value):
    count = len(first_end)
    diag = [None] + [last_end[i - 1] + first_end[i] for i in range(1, count)]
    load = [None] + [last_value[i - 1] - first_value[i] for i in range(1, count)]
    middle = count // 2
    inverse = [None] * count
    for i in range(1, middle):
        if i > 1:
            factor = across[i - 1] * inverse[i - 1]
            diag[i] = diag[i] - factor * across[i - 1]
            load[i] = load[i] + factor * load[i - 1]
        inverse[i] = 1.0 / diag[i]
    for i in range(count - 1, middle, -1):
        if i < count - 1:
            factor = across[i] * inverse[i + 1]
            diag[i] = diag[i] - factor * across[i]
            load[i] = load[i] + factor * load[i + 1]
        inverse[i] = 1.0 / diag[i]
    below = across[middle - 1] * inverse[middle - 1]
    above = across[middle] * inverse[middle + 1]
    diag[middle] = diag[middle] - below * across[middle - 1] - above * across[middle]
    load[middle] = load[middle] + below * load[middle - 1] + above * load[middle + 1]
    flux = [None] * count
    flux[middle] = load[middle] / diag[middle]
    for i in range(middle - 1, 0, -1):
        flux[i] = (load[i] + across[i] * flux[i + 1]) * inverse[i]
    for i in range(middle + 1, count):
        flux[i] = (load[i] + across[i - 1] * flux[i - 1]) * inverse[i]
    nothing = jnp.zeros_like(flux[middle])
    return [nothing] + flux[1:] + [nothing]


def side_lanes(rows, tests, from_left, from_right, own, side_part, side_first, side_last):
    halo = from_left[...] + from_right[...]
    mine = own[...]
    side_lane = lax.broadcasted_iota(jnp.int32, (rows, LANES), 1)
    outer = side_lane < 2 * tests
    halo_k = pltpu.roll(halo, LANES - 2 * tests, 1)
    own_k = pltpu.roll(mine, LANES - 2 * tests, 1)
    cond_s = jnp.where(outer, pltpu.roll(halo, LANES - 4 * tests, 1), own_k)
    cond_s = jnp.where(cond_s > 0.0, cond_s, 1.0)
    act_s = jnp.where(outer, pltpu.roll(halo, LANES - 6 * tests, 1), pltpu.roll(mine, LANES - 4 * tests, 1))
    side_face = (2.0 * explicit_ratio) * cond_s * halo_k / (cond_s + halo_k)
    given_s = jnp.where(outer, halo, act_s * side_face * (halo - mine))
    cond_sr = [cond_s[i : i + 1, :] for i in range(rows)]
    act_sr = [act_s[i : i + 1, :] for i in range(rows)]
    gains_s, inv_s, backs_s = eliminate(cond_sr, act_sr)
    first_s, last_s = responses(gains_s, inv_s, backs_s, act_sr)
    part_s = sweep(gains_s, inv_s, backs_s, [given_s[i : i + 1, :] for i in range(rows)])
    for i in range(rows):
        side_part[i : i + 1, :] = part_s[i]
        side_first[i : i + 1, :] = first_s[i]
        side_last[i : i + 1, :] = last_s[i]
    half = 0.5 / implicit_ratio
    ends = (
        part_s[0], part_s[-1], first_s[0] + half / cond_sr[0], last_s[-1] + half / cond_sr[-1], first_s[-1],
    )
    return ends


def line_kernel(devices, rows, tests, got, from_left, from_right, own, reply, side_part, side_first, side_last):
    def pick(low, high):
        return [got[d, low:high, :] for d in range(devices)]

    flux = chain(pick(16, 17), pick(17, 18), pick(18, 19), pick(0, tests), pick(tests, 2 * tests))
    ends = side_lanes(rows, tests, from_left, from_right, own, side_part, side_first, side_last)
    for d in range(devices):
        reply[d, 0:tests, :] = flux[d]
        reply[d, tests : 2 * tests, :] = flux[d + 1]
        for r, value in enumerate(ends):
            reply[d, 16 + r : 17 + r, :] = value


def final_kernel(
    rows, tests, hb, logk, heads_part, adjoint_part, first_in, last_in, got, from_left, from_right,
    side_part, side_first, side_last, heads, sensitivity, held,
):
    columns = hb.shape[1]
    tiles = columns // LANES
    devices = got.shape[0]
    side_rows = [[got[d, 16 + r : 17 + r, :] for d in range(devices)] for r in range(5)]
    for d, value in enumerate(chain(side_rows[2], side_rows[3], side_rows[4], side_rows[0], side_rows[1])):
        held[d : d + 1, :] = value
    me = lax.axis_index("gx")
    side_flux = [held[pl.ds(me, 1), :], held[pl.ds(me + 1, 1), :]]
    side = side_part[...] + side_first[...] * side_flux[0] - side_last[...] * side_flux[1]
    halo = from_left[...] + from_right[...]
    conduct = jnp.exp(logk[...])
    first = first_in[...]
    last = last_in[...]
    lane = lax.broadcasted_iota(jnp.int32, (rows, columns), 1)
    row = lax.broadcasted_iota(jnp.int32, (rows, columns), 0)
    at_start = lane == 0
    at_end = lane == columns - 1

    def wide(core, r):
        return jnp.concatenate([got[2 * k + core, r : r + 1, :] for k in range(tiles)], axis=1)

    def joined(part, t):
        starts = [k * tests * rows + t for k in range(tiles)]
        return jnp.concatenate([part[pl.ds(start, rows, stride=tests), :] for start in starts], axis=1)

    def beside(values, index):
        return values[:, index : index + 1]

    row_lane = lax.broadcasted_iota(jnp.int32, (1, columns), 1)
    end_products = [jnp.zeros((1, columns), jnp.float32)] * 2
    along_rows = jnp.zeros((rows, columns), jnp.float32)
    along_columns = jnp.zeros((rows, columns), jnp.float32)
    start_face = jnp.zeros((rows, LANES), jnp.float32)
    for t in range(tests):
        here = slice(rows * t, rows * (t + 1))
        fluxes = [[wide(core, base + t) for base in (0, tests)] for core in (0, 1)]
        head = joined(heads_part, t) + first * fluxes[0][0] - last * fluxes[0][1]
        head = head + jnp.where(at_start, beside(side, 2 * tests + t), 0.0)
        head = head + jnp.where(at_end, beside(side, 3 * tests + t), 0.0)
        heads[here, :] = head
        weight = joined(adjoint_part, t) + first * fluxes[1][0] - last * fluxes[1][1]
        for end in (0, 1):
            side_row = side_flux[end]
            whole = fluxes[0][end] + jnp.where(row_lane == 0, beside(side_row, 2 * tests + t), 0.0)
            whole = whole + jnp.where(row_lane == columns - 1, beside(side_row, 3 * tests + t), 0.0)
            end_products[end] = end_products[end] + whole * fluxes[1][end]
        east_head = pltpu.roll(head, rows - 1, 0)
        east_weight = pltpu.roll(weight, rows - 1, 0)
        along_rows = along_rows + (east_head - head) * (weight - east_weight)
        old = hb[here, :]
        north_old = jnp.where(at_end, beside(halo, 3 * tests + t), pltpu.roll(old, columns - 1, 1))
        north_weight = jnp.where(at_end, beside(side, tests + t), pltpu.roll(weight, columns - 1, 1))
        along_columns = along_columns + (north_old - old) * (weight - north_weight)
        start_face = start_face + (old[:, :LANES] - beside(halo, 2 * tests + t)) * (
            beside(side, t) - weight[:, :LANES]
        )
    cond_east = pltpu.roll(conduct, rows - 1, 0)
    face = 2.0 * conduct * cond_east / (conduct + cond_east)
    face = jnp.where(row == rows - 1, 0.0, face)
    share = implicit_ratio * face * face * along_rows
    total = share + pltpu.roll(share, 1, 0)
    cond_north = jnp.where(at_end, beside(halo, 5 * tests), pltpu.roll(conduct, columns - 1, 1))
    face = 2.0 * conduct * cond_north / (conduct + cond_north)
    share = explicit_ratio * face * face * along_columns
    cond_start = conduct[:, :LANES]
    cond_south = jnp.broadcast_to(beside(halo, 4 * tests), (rows, LANES))
    face = 2.0 * cond_start * cond_south / (cond_start + cond_south)
    start_share = explicit_ratio * face * face * start_face
    start_share = jnp.concatenate([start_share, jnp.zeros((rows, columns - LANES), jnp.float32)], axis=1)
    total = total + share + jnp.where(at_start, start_share, pltpu.roll(share, 1, 1))
    scale = -1.0 / implicit_ratio
    total = total + jnp.where(row == 0, scale * end_products[0], 0.0)
    total = total + jnp.where(row == rows - 1, scale * end_products[1], 0.0)
    sensitivity[...] = total * (0.5 / conduct)


def f32(*shape):
    return jax.ShapeDtypeStruct(shape, jnp.float32)


VMEM = pl.BlockSpec(memory_space=pltpu.VMEM)
SMEM = pl.BlockSpec(memory_space=pltpu.SMEM)
LOCAL_LIMIT = 58 * 1024 * 1024
PARAMS = pltpu.CompilerParams(vmem_limit_bytes=40 * 1024 * 1024)


def per_device(head_before, log_conductivity, fixed_mask, well_cells, pump_rates, adjoint_seed):
    tests, rows, columns = head_before.shape
    tiles = columns // LANES
    devices = lax.axis_size("gx")
    peers = lax.axis_size("gy")
    hb = head_before.reshape(tests * rows, columns)
    seed = adjoint_seed.reshape(tests * rows, columns)

    side = f32(rows, LANES)
    part = f32(tiles * tests * rows, LANES)
    anywhere = pl.BlockSpec(memory_space=pl.ANY)
    message, heads_part, adjoint_part, first, last, to_right, to_left, own = pl.pallas_call(
        functools.partial(local_kernel, rows, tests, columns * peers),
        in_specs=[SMEM] * 2 + [anywhere] * 4,
        out_specs=[VMEM] * 8,
        out_shape=[f32(devices, 24, LANES), part, part] + [f32(rows, columns)] * 2 + [side] * 3,
        scratch_shapes=[pltpu.VMEM((tests * rows, columns), jnp.float32)] * 2
        + [pltpu.VMEM((rows, columns), jnp.float32), pltpu.VMEM((rows, columns), jnp.int32)]
        + [pltpu.SemaphoreType.DMA((4,))]
        + [pltpu.VMEM((tiles * tests * rows, LANES), jnp.float32)] * 2
        + [pltpu.VMEM((rows * tiles, LANES), jnp.float32)] * 7,
        compiler_params=pltpu.CompilerParams(vmem_limit_bytes=LOCAL_LIMIT),
        name="local",
    )(well_cells, pump_rates, hb, seed, log_conductivity, fixed_mask)
    got = lax.all_to_all(message, "gx", 0, 0)
    from_left = lax.ppermute(to_right, "gy", [(i, i + 1) for i in range(peers - 1)])
    from_right = lax.ppermute(to_left, "gy", [(i + 1, i) for i in range(peers - 1)])
    reply, side_part, side_first, side_last = pl.pallas_call(
        functools.partial(line_kernel, devices, rows, tests),
        in_specs=[VMEM] * 4,
        out_specs=[VMEM] * 4,
        out_shape=[f32(devices, 24, LANES)] + [side] * 3,
        compiler_params=PARAMS,
        name="line",
    )(got, from_left, from_right, own)
    answer = lax.all_to_all(reply, "gx", 0, 0)
    heads, sensitivity = pl.pallas_call(
        functools.partial(final_kernel, rows, tests),
        in_specs=[VMEM] * 12,
        out_specs=[VMEM] * 2,
        out_shape=[f32(tests * rows, columns), f32(rows, columns)],
        scratch_shapes=[pltpu.VMEM((devices + SUBLANES, LANES), jnp.float32)],
        compiler_params=PARAMS,
        name="final",
    )(
        hb, log_conductivity, heads_part, adjoint_part, first, last, answer, from_left, from_right,
        side_part, side_first, side_last,
    )
    return heads.reshape(tests, rows, columns), sensitivity


def solution(mesh):
    return jax.shard_map(
        per_device,
        mesh=mesh,
        in_specs=(P(None, "gx", "gy"), P("gx", "gy"), P("gx", "gy"), P(), P(), P(None, "gx", "gy")),
        out_specs=(P(None, "gx", "gy"), P("gx", "gy")),
        check_vma=False,
    )
```

```python
import functools

import jax
import jax.numpy as jnp
from jax import lax
from jax.experimental import pallas as pl
from jax.experimental.pallas import tpu as pltpu
from jax.sharding import PartitionSpec as P

implicit_ratio = 4000.0
explicit_ratio = 0.1
LANES = 128
SUBLANES = 8


def spread_columns(lane, pieces):
    out = jnp.zeros(lane.shape, jnp.float32)
    for low, count, column in pieces:
        out = jnp.where((lane >= low) & (lane < low + count), column, out)
    return out


def edge_messages(rows, tests, hb, seed, conduct, active, to_right, to_left, own):
    columns = hb.shape[1]
    lane = lax.broadcasted_iota(jnp.int32, (rows, LANES), 1)
    sides = []
    for c in (0, columns - 1):
        column = slice(c, c + 1)
        heads = [hb[rows * t : rows * (t + 1), column] for t in range(tests)]
        seeds = [active[:, column] * seed[rows * t : rows * (t + 1), column] for t in range(tests)]
        sides.append((conduct[:, column], active[:, column], heads, seeds))

    def packed(side, odd, with_seed):
        conduct, active, heads, seeds = sides[side]
        base = tests * odd
        pieces = [(2 * tests + base + t, 1, heads[t]) for t in range(tests)]
        pieces += [(4 * tests + base, tests, conduct), (6 * tests + base, tests, active)]
        if with_seed:
            pieces += [(base + t, 1, seeds[t]) for t in range(tests)]
        return spread_columns(lane, pieces)

    to_right[...] = packed(1, 0, True)
    to_left[...] = packed(0, 1, True)
    own[...] = packed(0, 0, False) + packed(1, 1, False)


def eliminate(conduct, active):
    rows = len(conduct)
    gains, inverses, backs = [None], [], []
    excess = jnp.ones_like(conduct[0])
    face = None
    for i in range(rows):
        if i > 0:
            gain = active[i] * face * inverses[-1]
            gains.append(gain)
            excess = 1.0 + gain * excess
        if i < rows - 1:
            face = (2.0 * implicit_ratio) * conduct[i] * conduct[i + 1] / (conduct[i] + conduct[i + 1])
            upper = active[i] * face
            inverse = 1.0 / (excess + upper)
            backs.append(upper * inverse)
        else:
            inverse = 1.0 / excess
            backs.append(None)
        inverses.append(inverse)
    return gains, inverses, backs


def sweep(gains, inverses, backs, right):
    rows = len(right)
    held = [right[0]]
    for i in range(1, rows):
        held.append(right[i] + gains[i] * held[-1])
    values = [None] * rows
    values[-1] = held[-1] * inverses[-1]
    for i in range(rows - 2, -1, -1):
        values[i] = held[i] * inverses[i] + backs[i] * values[i + 1]
    return values


def responses(gains, inverses, backs, active):
    rows = len(active)
    held = [active[0]]
    for i in range(1, rows):
        held.append(gains[i] * held[-1])
    first, last = [None] * rows, [None] * rows
    first[-1] = held[-1] * inverses[-1]
    last[-1] = active[-1] * inverses[-1]
    for i in range(rows - 2, -1, -1):
        first[i] = held[i] * inverses[i] + backs[i] * first[i + 1]
        last[i] = backs[i] * last[i + 1]
    return first, last


def local_kernel(
    rows, tests, total_columns, wells_all, rates_all, hb_all, seed_all, logk_all, mask_all,
    message_all, heads_part, adjoint_part, first_out, last_out, to_right, to_left, own,
    wells, rates, hb, seed, logk, mask, message, arrived, taken, sent,
    right, weighed, cond_c, act_c, gain_c, inv_c, back_c, first_c, last_c,
):
    pairs = ((logk_all, logk), (mask_all, mask), (wells_all, wells), (rates_all, rates))
    copies = [pltpu.make_async_copy(whole, here, arrived.at[n]) for n, (whole, here) in enumerate(pairs)]
    for t in range(tests):
        here = pl.ds(rows * t, rows)
        for n, (whole, part) in enumerate(((hb_all, hb), (seed_all, seed))):
            copies.append(pltpu.make_async_copy(whole.at[here, :], part.at[here, :], taken.at[n, t]))
    for copy in copies:
        copy.start()
    columns = hb.shape[1]
    tiles = columns // LANES
    field = tests * rows
    copies[0].wait()
    copies[1].wait()
    conduct = jnp.exp(logk[...])
    active = (1 - mask[...]).astype(jnp.float32)
    for k in range(tiles):
        cond_c[pl.ds(k, rows, stride=tiles), :] = conduct[:, k * LANES : (k + 1) * LANES]
        act_c[pl.ds(k, rows, stride=tiles), :] = active[:, k * LANES : (k + 1) * LANES]
    cond_rows = [cond_c[tiles * i : tiles * (i + 1), :] for i in range(rows)]
    act_rows = [act_c[tiles * i : tiles * (i + 1), :] for i in range(rows)]
    gains, inverses, backs = eliminate(cond_rows, act_rows)
    first, last = responses(gains, inverses, backs, act_rows)
    for i in range(rows):
        here = slice(tiles * i, tiles * (i + 1))
        if i > 0:
            gain_c[here, :] = gains[i]
        inv_c[here, :] = inverses[i]
        if i < rows - 1:
            back_c[here, :] = backs[i]
        first_c[here, :] = first[i]
        last_c[here, :] = last[i]
    half = 0.5 / implicit_ratio
    first_end = first[0] + half / cond_rows[0]
    last_end = last[-1] + half / cond_rows[-1]
    across = first[-1]

    lane = lax.broadcasted_iota(jnp.int32, (rows, columns), 1)
    cond_north = pltpu.roll(conduct, columns - 1, 1)
    face = (2.0 * explicit_ratio) * conduct * cond_north / (conduct + cond_north)
    face = jnp.where(lane == columns - 1, 0.0, face)
    for t in range(tests):
        here = slice(rows * t, rows * (t + 1))
        copies[4 + 2 * t].wait()
        copies[5 + 2 * t].wait()
        head = hb[here, :]
        flow = face * (pltpu.roll(head, columns - 1, 1) - head)
        value = head + active * (flow - pltpu.roll(flow, 1, 1))
        seeded = active * seed[here, :]
        for k in range(tiles):
            lanes = slice(k * LANES, (k + 1) * LANES)
            there = slice(k * field + rows * t, k * field + rows * (t + 1))
            right[there, :] = value[:, lanes]
            weighed[there, :] = seeded[:, lanes]
    copies[2].wait()
    copies[3].wait()
    row_start = lax.axis_index("gx") * rows
    column_start = lax.axis_index("gy") * columns
    row_lane = lax.broadcasted_iota(jnp.int32, (1, LANES), 1)
    for t in range(tests):
        well = wells[t]
        well_row = well // total_columns - row_start
        well_column = well % total_columns - column_start
        inside = (well_row >= 0) & (well_row < rows) & (well_column >= 0) & (well_column < columns)

        @pl.when(inside)
        def _():
            tile = well_column // LANES
            act_row = act_c[pl.ds(tiles * well_row + tile, 1), :]
            there = pl.ds(tile * field + rows * t + well_row, 1)
            added = jnp.where(row_lane == well_column % LANES, act_row * rates[t], 0.0)
            right[there, :] = right[there, :] + added

    sending = []
    for k in range(tiles):
        lanes = slice(k * LANES, (k + 1) * LANES)
        gain_k = [None] + [gain_c[tiles * i + k : tiles * i + k + 1, :] for i in range(1, rows)]
        inv_k = [inv_c[tiles * i + k : tiles * i + k + 1, :] for i in range(rows)]
        back_k = [back_c[tiles * i + k : tiles * i + k + 1, :] for i in range(rows - 1)] + [None]
        for core, (source, out) in enumerate(((right, heads_part), (weighed, adjoint_part))):
            given = [source[pl.ds(k * field + i, tests, stride=rows), :] for i in range(rows)]
            values = sweep(gain_k, inv_k, back_k, given)
            for i in range(rows):
                start = k * field + i * tests
                out[start : start + tests, :] = values[i]
            dest = 2 * k + core
            message[dest, 0:tests, :] = values[0]
            message[dest, tests : 2 * tests, :] = values[-1]
            message[dest, 16:17, :] = first_end[k : k + 1, :]
            message[dest, 17:18, :] = last_end[k : k + 1, :]
            message[dest, 18:19, :] = across[k : k + 1, :]
        both = pl.ds(2 * k, 2)
        sending.append(pltpu.make_async_copy(message.at[both], message_all.at[both], sent.at[k]))
        sending[-1].start()
        first_out[:, lanes] = first_c[pl.ds(k, rows, stride=tiles), :]
        last_out[:, lanes] = last_c[pl.ds(k, rows, stride=tiles), :]
    edge_messages(rows, tests, hb, seed, conduct, active, to_right, to_left, own)
    for copy in sending:
        copy.wait()


def chain(first_end, last_end, across, first_value, last_value):
    count = len(first_end)
    diag = [None] + [last_end[i - 1] + first_end[i] for i in range(1, count)]
    load = [None] + [last_value[i - 1] - first_value[i] for i in range(1, count)]
    middle = count // 2
    inverse = [None] * count
    for i in range(1, middle):
        if i > 1:
            factor = across[i - 1] * inverse[i - 1]
            diag[i] = diag[i] - factor * across[i - 1]
            load[i] = load[i] + factor * load[i - 1]
        inverse[i] = 1.0 / diag[i]
    for i in range(count - 1, middle, -1):
        if i < count - 1:
            factor = across[i] * inverse[i + 1]
            diag[i] = diag[i] - factor * across[i]
            load[i] = load[i] + factor * load[i + 1]
        inverse[i] = 1.0 / diag[i]
    below = across[middle - 1] * inverse[middle - 1]
    above = across[middle] * inverse[middle + 1]
    diag[middle] = diag[middle] - below * across[middle - 1] - above * across[middle]
    load[middle] = load[middle] + below * load[middle - 1] + above * load[middle + 1]
    flux = [None] * count
    flux[middle] = load[middle] / diag[middle]
    for i in range(middle - 1, 0, -1):
        flux[i] = (load[i] + across[i] * flux[i + 1]) * inverse[i]
    for i in range(middle + 1, count):
        flux[i] = (load[i] + across[i - 1] * flux[i - 1]) * inverse[i]
    nothing = jnp.zeros_like(flux[middle])
    return [nothing] + flux[1:] + [nothing]


def side_lanes(rows, tests, from_left, from_right, own, side_part, side_first, side_last):
    halo = from_left[...] + from_right[...]
    mine = own[...]
    side_lane = lax.broadcasted_iota(jnp.int32, (rows, LANES), 1)
    outer = side_lane < 2 * tests
    halo_k = pltpu.roll(halo, LANES - 2 * tests, 1)
    own_k = pltpu.roll(mine, LANES - 2 * tests, 1)
    cond_s = jnp.where(outer, pltpu.roll(halo, LANES - 4 * tests, 1), own_k)
    cond_s = jnp.where(cond_s > 0.0, cond_s, 1.0)
    act_s = jnp.where(outer, pltpu.roll(halo, LANES - 6 * tests, 1), pltpu.roll(mine, LANES - 4 * tests, 1))
    side_face = (2.0 * explicit_ratio) * cond_s * halo_k / (cond_s + halo_k)
    given_s = jnp.where(outer, halo, act_s * side_face * (halo - mine))
    cond_sr = [cond_s[i : i + 1, :] for i in range(rows)]
    act_sr = [act_s[i : i + 1, :] for i in range(rows)]
    gains_s, inv_s, backs_s = eliminate(cond_sr, act_sr)
    first_s, last_s = responses(gains_s, inv_s, backs_s, act_sr)
    part_s = sweep(gains_s, inv_s, backs_s, [given_s[i : i + 1, :] for i in range(rows)])
    for i in range(rows):
        side_part[i : i + 1, :] = part_s[i]
        side_first[i : i + 1, :] = first_s[i]
        side_last[i : i + 1, :] = last_s[i]
    half = 0.5 / implicit_ratio
    ends = (
        part_s[0], part_s[-1], first_s[0] + half / cond_sr[0], last_s[-1] + half / cond_sr[-1], first_s[-1],
    )
    return ends


def line_kernel(devices, rows, tests, got, from_left, from_right, own, reply, side_part, side_first, side_last):
    def pick(low, high):
        return [got[d, low:high, :] for d in range(devices)]

    flux = chain(pick(16, 17), pick(17, 18), pick(18, 19), pick(0, tests), pick(tests, 2 * tests))
    ends = side_lanes(rows, tests, from_left, from_right, own, side_part, side_first, side_last)
    for d in range(devices):
        reply[d, 0:tests, :] = flux[d]
        reply[d, tests : 2 * tests, :] = flux[d + 1]
        for r, value in enumerate(ends):
            reply[d, 16 + r : 17 + r, :] = value


def final_kernel(
    rows, tests, hb, logk, heads_part, adjoint_part, first_in, last_in, got, from_left, from_right,
    side_part, side_first, side_last, heads_all, sensitivity, heads, sent, held,
):
    columns = hb.shape[1]
    tiles = columns // LANES
    devices = got.shape[0]
    side_rows = [[got[d, 16 + r : 17 + r, :] for d in range(devices)] for r in range(5)]
    for d, value in enumerate(chain(side_rows[2], side_rows[3], side_rows[4], side_rows[0], side_rows[1])):
        held[d : d + 1, :] = value
    me = lax.axis_index("gx")
    side_flux = [held[pl.ds(me, 1), :], held[pl.ds(me + 1, 1), :]]
    side = side_part[...] + side_first[...] * side_flux[0] - side_last[...] * side_flux[1]
    halo = from_left[...] + from_right[...]
    conduct = jnp.exp(logk[...])
    first = first_in[...]
    last = last_in[...]
    lane = lax.broadcasted_iota(jnp.int32, (rows, columns), 1)
    row = lax.broadcasted_iota(jnp.int32, (rows, columns), 0)
    at_start = lane == 0
    at_end = lane == columns - 1

    def wide(core, r):
        return jnp.concatenate([got[2 * k + core, r : r + 1, :] for k in range(tiles)], axis=1)

    def joined(part, t):
        starts = [k * tests * rows + t for k in range(tiles)]
        return jnp.concatenate([part[pl.ds(start, rows, stride=tests), :] for start in starts], axis=1)

    def beside(values, index):
        return values[:, index : index + 1]

    row_lane = lax.broadcasted_iota(jnp.int32, (1, columns), 1)
    end_products = [jnp.zeros((1, columns), jnp.float32)] * 2
    along_rows = jnp.zeros((rows, columns), jnp.float32)
    along_columns = jnp.zeros((rows, columns), jnp.float32)
    start_face = jnp.zeros((rows, LANES), jnp.float32)
    sending = []
    for t in range(tests):
        here = slice(rows * t, rows * (t + 1))
        block = pl.ds(rows * t, rows)
        fluxes = [[wide(core, base + t) for base in (0, tests)] for core in (0, 1)]
        head = joined(heads_part, t) + first * fluxes[0][0] - last * fluxes[0][1]
        head = head + jnp.where(at_start, beside(side, 2 * tests + t), 0.0)
        head = head + jnp.where(at_end, beside(side, 3 * tests + t), 0.0)
        heads[here, :] = head
        sending.append(pltpu.make_async_copy(heads.at[block, :], heads_all.at[block, :], sent.at[t]))
        sending[-1].start()
        weight = joined(adjoint_part, t) + first * fluxes[1][0] - last * fluxes[1][1]
        for end in (0, 1):
            side_row = side_flux[end]
            whole = fluxes[0][end] + jnp.where(row_lane == 0, beside(side_row, 2 * tests + t), 0.0)
            whole = whole + jnp.where(row_lane == columns - 1, beside(side_row, 3 * tests + t), 0.0)
            end_products[end] = end_products[end] + whole * fluxes[1][end]
        east_head = pltpu.roll(head, rows - 1, 0)
        east_weight = pltpu.roll(weight, rows - 1, 0)
        along_rows = along_rows + (east_head - head) * (weight - east_weight)
        old = hb[here, :]
        north_old = jnp.where(at_end, beside(halo, 3 * tests + t), pltpu.roll(old, columns - 1, 1))
        north_weight = jnp.where(at_end, beside(side, tests + t), pltpu.roll(weight, columns - 1, 1))
        along_columns = along_columns + (north_old - old) * (weight - north_weight)
        start_face = start_face + (old[:, :LANES] - beside(halo, 2 * tests + t)) * (
            beside(side, t) - weight[:, :LANES]
        )
    cond_east = pltpu.roll(conduct, rows - 1, 0)
    face = 2.0 * conduct * cond_east / (conduct + cond_east)
    face = jnp.where(row == rows - 1, 0.0, face)
    share = implicit_ratio * face * face * along_rows
    total = share + pltpu.roll(share, 1, 0)
    cond_north = jnp.where(at_end, beside(halo, 5 * tests), pltpu.roll(conduct, columns - 1, 1))
    face = 2.0 * conduct * cond_north / (conduct + cond_north)
    share = explicit_ratio * face * face * along_columns
    cond_start = conduct[:, :LANES]
    cond_south = jnp.broadcast_to(beside(halo, 4 * tests), (rows, LANES))
    face = 2.0 * cond_start * cond_south / (cond_start + cond_south)
    start_share = explicit_ratio * face * face * start_face
    start_share = jnp.concatenate([start_share, jnp.zeros((rows, columns - LANES), jnp.float32)], axis=1)
    total = total + share + jnp.where(at_start, start_share, pltpu.roll(share, 1, 1))
    scale = -1.0 / implicit_ratio
    total = total + jnp.where(row == 0, scale * end_products[0], 0.0)
    total = total + jnp.where(row == rows - 1, scale * end_products[1], 0.0)
    sensitivity[...] = total * (0.5 / conduct)
    for copy in sending:
        copy.wait()


def in_hbm(x):
    return pltpu.with_memory_space_constraint(x, pltpu.HBM)


def f32(*shape):
    return jax.ShapeDtypeStruct(shape, jnp.float32)


VMEM = pl.BlockSpec(memory_space=pltpu.VMEM)
PARAMS = pltpu.CompilerParams(vmem_limit_bytes=40 * 1024 * 1024)


def per_device(head_before, log_conductivity, fixed_mask, well_cells, pump_rates, adjoint_seed):
    tests, rows, columns = head_before.shape
    tiles = columns // LANES
    devices = lax.axis_size("gx")
    peers = lax.axis_size("gy")
    hb = head_before.reshape(tests * rows, columns)
    seed = adjoint_seed.reshape(tests * rows, columns)

    side = f32(rows, LANES)
    part = f32(tiles * tests * rows, LANES)
    anywhere = pl.BlockSpec(memory_space=pl.ANY)
    message, heads_part, adjoint_part, first, last, to_right, to_left, own = pl.pallas_call(
        functools.partial(local_kernel, rows, tests, columns * peers),
        in_specs=[anywhere] * 6,
        out_specs=[anywhere] + [VMEM] * 7,
        out_shape=[f32(devices, 24, LANES), part, part] + [f32(rows, columns)] * 2 + [side] * 3,
        scratch_shapes=[pltpu.SMEM((tests,), jnp.int32), pltpu.SMEM((tests,), jnp.float32)]
        + [pltpu.VMEM((tests * rows, columns), jnp.float32)] * 2
        + [pltpu.VMEM((rows, columns), jnp.float32), pltpu.VMEM((rows, columns), jnp.int32)]
        + [pltpu.VMEM((devices, 24, LANES), jnp.float32)]
        + [pltpu.SemaphoreType.DMA((4,)), pltpu.SemaphoreType.DMA((2, tests)), pltpu.SemaphoreType.DMA((tiles,))]
        + [pltpu.VMEM((tiles * tests * rows, LANES), jnp.float32)] * 2
        + [pltpu.VMEM((rows * tiles, LANES), jnp.float32)] * 7,
        compiler_params=PARAMS,
        name="local",
    )(*[in_hbm(x) for x in (well_cells, pump_rates, hb, seed, log_conductivity, fixed_mask)])
    got = lax.all_to_all(message, "gx", 0, 0)
    from_left = lax.ppermute(to_right, "gy", [(i, i + 1) for i in range(peers - 1)])
    from_right = lax.ppermute(to_left, "gy", [(i + 1, i) for i in range(peers - 1)])
    reply, side_part, side_first, side_last = pl.pallas_call(
        functools.partial(line_kernel, devices, rows, tests),
        in_specs=[VMEM] * 4,
        out_specs=[VMEM] * 4,
        out_shape=[f32(devices, 24, LANES)] + [side] * 3,
        compiler_params=PARAMS,
        name="line",
    )(got, from_left, from_right, own)
    answer = lax.all_to_all(reply, "gx", 0, 0)
    heads, sensitivity = pl.pallas_call(
        functools.partial(final_kernel, rows, tests),
        in_specs=[VMEM] * 12,
        out_specs=[anywhere, VMEM],
        out_shape=[f32(tests * rows, columns), f32(rows, columns)],
        scratch_shapes=[pltpu.VMEM((tests * rows, columns), jnp.float32), pltpu.SemaphoreType.DMA((tests,))]
        + [pltpu.VMEM((devices + SUBLANES, LANES), jnp.float32)],
        compiler_params=PARAMS,
        name="final",
    )(
        hb, log_conductivity, heads_part, adjoint_part, first, last, answer, from_left, from_right,
        side_part, side_first, side_last,
    )
    return heads.reshape(tests, rows, columns), sensitivity


def solution(mesh):
    return jax.shard_map(
        per_device,
        mesh=mesh,
        in_specs=(P(None, "gx", "gy"), P("gx", "gy"), P("gx", "gy"), P(), P(), P(None, "gx", "gy")),
        out_specs=(P(None, "gx", "gy"), P("gx", "gy")),
        check_vma=False,
    )
```

```python
import functools

import jax
import jax.numpy as jnp
from jax import lax
from jax.experimental import pallas as pl
from jax.experimental.pallas import tpu as pltpu
from jax.sharding import PartitionSpec as P

implicit_ratio = 4000.0
explicit_ratio = 0.1
LANES = 128
SUBLANES = 8


def spread_columns(lane, pieces):
    out = jnp.zeros(lane.shape, jnp.float32)
    for low, count, column in pieces:
        out = jnp.where((lane >= low) & (lane < low + count), column, out)
    return out


def edge_messages(rows, tests, hb, seed, conduct, active, to_right, to_left, own):
    columns = hb.shape[1]
    lane = lax.broadcasted_iota(jnp.int32, (rows, LANES), 1)
    sides = []
    for c in (0, columns - 1):
        column = slice(c, c + 1)
        heads = [hb[rows * t : rows * (t + 1), column] for t in range(tests)]
        seeds = [active[:, column] * seed[rows * t : rows * (t + 1), column] for t in range(tests)]
        sides.append((conduct[:, column], active[:, column], heads, seeds))

    def packed(side, odd, with_seed):
        conduct, active, heads, seeds = sides[side]
        base = tests * odd
        pieces = [(2 * tests + base + t, 1, heads[t]) for t in range(tests)]
        pieces += [(4 * tests + base, tests, conduct), (6 * tests + base, tests, active)]
        if with_seed:
            pieces += [(base + t, 1, seeds[t]) for t in range(tests)]
        return spread_columns(lane, pieces)

    to_right[...] = packed(1, 0, True)
    to_left[...] = packed(0, 1, True)
    own[...] = packed(0, 0, False) + packed(1, 1, False)


def eliminate(conduct, active):
    rows = len(conduct)
    gains, inverses, backs = [None], [], []
    excess = jnp.ones_like(conduct[0])
    face = None
    for i in range(rows):
        if i > 0:
            gain = active[i] * face * inverses[-1]
            gains.append(gain)
            excess = 1.0 + gain * excess
        if i < rows - 1:
            face = (2.0 * implicit_ratio) * conduct[i] * conduct[i + 1] / (conduct[i] + conduct[i + 1])
            upper = active[i] * face
            inverse = 1.0 / (excess + upper)
            backs.append(upper * inverse)
        else:
            inverse = 1.0 / excess
            backs.append(None)
        inverses.append(inverse)
    return gains, inverses, backs


def sweep(gains, inverses, backs, right):
    rows = len(right)
    held = [right[0]]
    for i in range(1, rows):
        held.append(right[i] + gains[i] * held[-1])
    values = [None] * rows
    values[-1] = held[-1] * inverses[-1]
    for i in range(rows - 2, -1, -1):
        values[i] = held[i] * inverses[i] + backs[i] * values[i + 1]
    return values


def responses(gains, inverses, backs, active):
    rows = len(active)
    held = [active[0]]
    for i in range(1, rows):
        held.append(gains[i] * held[-1])
    first, last = [None] * rows, [None] * rows
    first[-1] = held[-1] * inverses[-1]
    last[-1] = active[-1] * inverses[-1]
    for i in range(rows - 2, -1, -1):
        first[i] = held[i] * inverses[i] + backs[i] * first[i + 1]
        last[i] = backs[i] * last[i + 1]
    return first, last


def local_kernel(
    rows, tests, total_columns, wells_all, rates_all, hb_all, seed_all, logk_all, mask_all,
    message_all, heads_part, adjoint_part, first_out, last_out, to_right, to_left, own,
    wells, rates, hb, seed, logk, mask, message, arrived, sent,
    right, weighed, cond_c, act_c, gain_c, inv_c, back_c, first_c, last_c,
):
    pairs = (
        (logk_all, logk), (mask_all, mask), (hb_all, hb), (seed_all, seed), (wells_all, wells), (rates_all, rates),
    )
    copies = [pltpu.make_async_copy(whole, here, arrived.at[n]) for n, (whole, here) in enumerate(pairs)]
    for copy in copies:
        copy.start()
    columns = hb.shape[1]
    tiles = columns // LANES
    field = tests * rows
    copies[0].wait()
    copies[1].wait()
    conduct = jnp.exp(logk[...])
    active = (1 - mask[...]).astype(jnp.float32)
    for k in range(tiles):
        cond_c[pl.ds(k, rows, stride=tiles), :] = conduct[:, k * LANES : (k + 1) * LANES]
        act_c[pl.ds(k, rows, stride=tiles), :] = active[:, k * LANES : (k + 1) * LANES]
    cond_rows = [cond_c[tiles * i : tiles * (i + 1), :] for i in range(rows)]
    act_rows = [act_c[tiles * i : tiles * (i + 1), :] for i in range(rows)]
    gains, inverses, backs = eliminate(cond_rows, act_rows)
    first, last = responses(gains, inverses, backs, act_rows)
    for i in range(rows):
        here = slice(tiles * i, tiles * (i + 1))
        if i > 0:
            gain_c[here, :] = gains[i]
        inv_c[here, :] = inverses[i]
        if i < rows - 1:
            back_c[here, :] = backs[i]
        first_c[here, :] = first[i]
        last_c[here, :] = last[i]
    half = 0.5 / implicit_ratio
    first_end = first[0] + half / cond_rows[0]
    last_end = last[-1] + half / cond_rows[-1]
    across = first[-1]

    copies[2].wait()
    copies[3].wait()
    lane = lax.broadcasted_iota(jnp.int32, (rows, columns), 1)
    cond_north = pltpu.roll(conduct, columns - 1, 1)
    face = (2.0 * explicit_ratio) * conduct * cond_north / (conduct + cond_north)
    face = jnp.where(lane == columns - 1, 0.0, face)
    for t in range(tests):
        here = slice(rows * t, rows * (t + 1))
        head = hb[here, :]
        flow = face * (pltpu.roll(head, columns - 1, 1) - head)
        value = head + active * (flow - pltpu.roll(flow, 1, 1))
        seeded = active * seed[here, :]
        for k in range(tiles):
            lanes = slice(k * LANES, (k + 1) * LANES)
            there = slice(k * field + rows * t, k * field + rows * (t + 1))
            right[there, :] = value[:, lanes]
            weighed[there, :] = seeded[:, lanes]
    copies[4].wait()
    copies[5].wait()
    row_start = lax.axis_index("gx") * rows
    column_start = lax.axis_index("gy") * columns
    row_lane = lax.broadcasted_iota(jnp.int32, (1, LANES), 1)
    for t in range(tests):
        well = wells[t]
        well_row = well // total_columns - row_start
        well_column = well % total_columns - column_start
        inside = (well_row >= 0) & (well_row < rows) & (well_column >= 0) & (well_column < columns)

        @pl.when(inside)
        def _():
            tile = well_column // LANES
            act_row = act_c[pl.ds(tiles * well_row + tile, 1), :]
            there = pl.ds(tile * field + rows * t + well_row, 1)
            added = jnp.where(row_lane == well_column % LANES, act_row * rates[t], 0.0)
            right[there, :] = right[there, :] + added

    for k in range(tiles):
        lanes = slice(k * LANES, (k + 1) * LANES)
        gain_k = [None] + [gain_c[tiles * i + k : tiles * i + k + 1, :] for i in range(1, rows)]
        inv_k = [inv_c[tiles * i + k : tiles * i + k + 1, :] for i in range(rows)]
        back_k = [back_c[tiles * i + k : tiles * i + k + 1, :] for i in range(rows - 1)] + [None]
        for core, (source, out) in enumerate(((right, heads_part), (weighed, adjoint_part))):
            given = [source[pl.ds(k * field + i, tests, stride=rows), :] for i in range(rows)]
            values = sweep(gain_k, inv_k, back_k, given)
            for i in range(rows):
                start = k * field + i * tests
                out[start : start + tests, :] = values[i]
            start = (2 * k + core) * (2 * tests + 3)
            message[start : start + tests, :] = values[0]
            message[start + tests : start + 2 * tests, :] = values[-1]
            for r, value in enumerate((first_end, last_end, across)):
                message[start + 2 * tests + r : start + 2 * tests + r + 1, :] = value[k : k + 1, :]
        first_out[:, lanes] = first_c[pl.ds(k, rows, stride=tiles), :]
        last_out[:, lanes] = last_c[pl.ds(k, rows, stride=tiles), :]
    sending = pltpu.make_async_copy(message, message_all, sent)
    sending.start()
    edge_messages(rows, tests, hb, seed, conduct, active, to_right, to_left, own)
    sending.wait()


def chain(first_end, last_end, across, first_value, last_value):
    count = len(first_end)
    diag = [None] + [last_end[i - 1] + first_end[i] for i in range(1, count)]
    load = [None] + [last_value[i - 1] - first_value[i] for i in range(1, count)]
    middle = count // 2
    inverse = [None] * count
    for i in range(1, middle):
        if i > 1:
            factor = across[i - 1] * inverse[i - 1]
            diag[i] = diag[i] - factor * across[i - 1]
            load[i] = load[i] + factor * load[i - 1]
        inverse[i] = 1.0 / diag[i]
    for i in range(count - 1, middle, -1):
        if i < count - 1:
            factor = across[i] * inverse[i + 1]
            diag[i] = diag[i] - factor * across[i]
            load[i] = load[i] + factor * load[i + 1]
        inverse[i] = 1.0 / diag[i]
    below = across[middle - 1] * inverse[middle - 1]
    above = across[middle] * inverse[middle + 1]
    diag[middle] = diag[middle] - below * across[middle - 1] - above * across[middle]
    load[middle] = load[middle] + below * load[middle - 1] + above * load[middle + 1]
    flux = [None] * count
    flux[middle] = load[middle] / diag[middle]
    for i in range(middle - 1, 0, -1):
        flux[i] = (load[i] + across[i] * flux[i + 1]) * inverse[i]
    for i in range(middle + 1, count):
        flux[i] = (load[i] + across[i - 1] * flux[i - 1]) * inverse[i]
    nothing = jnp.zeros_like(flux[middle])
    return [nothing] + flux[1:] + [nothing]


def side_lanes(rows, tests, from_left, from_right, own, side_part, side_first, side_last):
    halo = from_left[...] + from_right[...]
    mine = own[...]
    side_lane = lax.broadcasted_iota(jnp.int32, (rows, LANES), 1)
    outer = side_lane < 2 * tests
    halo_k = pltpu.roll(halo, LANES - 2 * tests, 1)
    own_k = pltpu.roll(mine, LANES - 2 * tests, 1)
    cond_s = jnp.where(outer, pltpu.roll(halo, LANES - 4 * tests, 1), own_k)
    cond_s = jnp.where(cond_s > 0.0, cond_s, 1.0)
    act_s = jnp.where(outer, pltpu.roll(halo, LANES - 6 * tests, 1), pltpu.roll(mine, LANES - 4 * tests, 1))
    side_face = (2.0 * explicit_ratio) * cond_s * halo_k / (cond_s + halo_k)
    given_s = jnp.where(outer, halo, act_s * side_face * (halo - mine))
    cond_sr = [cond_s[i : i + 1, :] for i in range(rows)]
    act_sr = [act_s[i : i + 1, :] for i in range(rows)]
    gains_s, inv_s, backs_s = eliminate(cond_sr, act_sr)
    first_s, last_s = responses(gains_s, inv_s, backs_s, act_sr)
    part_s = sweep(gains_s, inv_s, backs_s, [given_s[i : i + 1, :] for i in range(rows)])
    for i in range(rows):
        side_part[i : i + 1, :] = part_s[i]
        side_first[i : i + 1, :] = first_s[i]
        side_last[i : i + 1, :] = last_s[i]
    half = 0.5 / implicit_ratio
    ends = (
        part_s[0], part_s[-1], first_s[0] + half / cond_sr[0], last_s[-1] + half / cond_sr[-1], first_s[-1],
    )
    return ends


def line_kernel(devices, rows, tests, got, from_left, from_right, own, reply, side_part, side_first, side_last):
    out_rows, back_rows = 2 * tests + 3, 2 * tests + 2

    def pick(low, high):
        return [got[out_rows * d + low : out_rows * d + high, :] for d in range(devices)]

    ends = [pick(2 * tests + r, 2 * tests + r + 1) for r in range(3)]
    flux = chain(*ends, pick(0, tests), pick(tests, 2 * tests))
    side = side_lanes(rows, tests, from_left, from_right, own, side_part, side_first, side_last)
    width = 4 * tests
    lane = lax.broadcasted_iota(jnp.int32, (1, LANES), 1)
    joined = side[0]
    for r in range(1, 4):
        joined = jnp.where(lane >= width * r, pltpu.roll(side[r], width * r, 1), joined)
    for d in range(devices):
        start = back_rows * d
        reply[start : start + tests, :] = flux[d]
        reply[start + tests : start + 2 * tests, :] = flux[d + 1]
        reply[start + 2 * tests : start + 2 * tests + 1, :] = joined
        reply[start + 2 * tests + 1 : start + back_rows, :] = side[4]


def final_kernel(
    rows, tests, hb, logk, heads_part, adjoint_part, first_in, last_in, got, from_left, from_right,
    side_part, side_first, side_last, heads, sensitivity, held,
):
    columns = hb.shape[1]
    tiles = columns // LANES
    back_rows = 2 * tests + 2
    devices = got.shape[0] // back_rows
    width = 4 * tests

    def sent_row(r):
        return jnp.concatenate([got[back_rows * d + r : back_rows * d + r + 1, :] for d in range(devices)], axis=0)

    packed = sent_row(2 * tests)
    ends = [packed] + [pltpu.roll(packed, LANES - width * r, 1) for r in range(1, 4)] + [sent_row(2 * tests + 1)]
    ends = [[value[d : d + 1, :] for d in range(devices)] for value in ends]
    for d, value in enumerate(chain(ends[2], ends[3], ends[4], ends[0], ends[1])):
        held[d : d + 1, :] = value
    me = lax.axis_index("gx")
    side_flux = [held[pl.ds(me, 1), :], held[pl.ds(me + 1, 1), :]]
    side = side_part[...] + side_first[...] * side_flux[0] - side_last[...] * side_flux[1]
    halo = from_left[...] + from_right[...]
    conduct = jnp.exp(logk[...])
    first = first_in[...]
    last = last_in[...]
    lane = lax.broadcasted_iota(jnp.int32, (rows, columns), 1)
    row = lax.broadcasted_iota(jnp.int32, (rows, columns), 0)
    at_start = lane == 0
    at_end = lane == columns - 1

    def wide(core, r):
        starts = [back_rows * (2 * k + core) for k in range(tiles)]
        return jnp.concatenate([got[starts[k] + r : starts[k] + r + 1, :] for k in range(tiles)], axis=1)

    def joined(part, t):
        starts = [k * tests * rows + t for k in range(tiles)]
        return jnp.concatenate([part[pl.ds(start, rows, stride=tests), :] for start in starts], axis=1)

    def beside(values, index):
        return values[:, index : index + 1]

    row_lane = lax.broadcasted_iota(jnp.int32, (1, columns), 1)
    end_products = [jnp.zeros((1, columns), jnp.float32)] * 2
    along_rows = jnp.zeros((rows, columns), jnp.float32)
    along_columns = jnp.zeros((rows, columns), jnp.float32)
    start_face = jnp.zeros((rows, LANES), jnp.float32)
    for t in range(tests):
        here = slice(rows * t, rows * (t + 1))
        fluxes = [[wide(core, base + t) for base in (0, tests)] for core in (0, 1)]
        head = joined(heads_part, t) + first * fluxes[0][0] - last * fluxes[0][1]
        head = head + jnp.where(at_start, beside(side, 2 * tests + t), 0.0)
        head = head + jnp.where(at_end, beside(side, 3 * tests + t), 0.0)
        heads[here, :] = head
        weight = joined(adjoint_part, t) + first * fluxes[1][0] - last * fluxes[1][1]
        for end in (0, 1):
            side_row = side_flux[end]
            whole = fluxes[0][end] + jnp.where(row_lane == 0, beside(side_row, 2 * tests + t), 0.0)
            whole = whole + jnp.where(row_lane == columns - 1, beside(side_row, 3 * tests + t), 0.0)
            end_products[end] = end_products[end] + whole * fluxes[1][end]
        east_head = pltpu.roll(head, rows - 1, 0)
        east_weight = pltpu.roll(weight, rows - 1, 0)
        along_rows = along_rows + (east_head - head) * (weight - east_weight)
        old = hb[here, :]
        north_old = jnp.where(at_end, beside(halo, 3 * tests + t), pltpu.roll(old, columns - 1, 1))
        north_weight = jnp.where(at_end, beside(side, tests + t), pltpu.roll(weight, columns - 1, 1))
        along_columns = along_columns + (north_old - old) * (weight - north_weight)
        start_face = start_face + (old[:, :LANES] - beside(halo, 2 * tests + t)) * (
            beside(side, t) - weight[:, :LANES]
        )
    cond_east = pltpu.roll(conduct, rows - 1, 0)
    face = 2.0 * conduct * cond_east / (conduct + cond_east)
    face = jnp.where(row == rows - 1, 0.0, face)
    share = implicit_ratio * face * face * along_rows
    total = share + pltpu.roll(share, 1, 0)
    cond_north = jnp.where(at_end, beside(halo, 5 * tests), pltpu.roll(conduct, columns - 1, 1))
    face = 2.0 * conduct * cond_north / (conduct + cond_north)
    share = explicit_ratio * face * face * along_columns
    cond_start = conduct[:, :LANES]
    cond_south = jnp.broadcast_to(beside(halo, 4 * tests), (rows, LANES))
    face = 2.0 * cond_start * cond_south / (cond_start + cond_south)
    start_share = explicit_ratio * face * face * start_face
    start_share = jnp.concatenate([start_share, jnp.zeros((rows, columns - LANES), jnp.float32)], axis=1)
    total = total + share + jnp.where(at_start, start_share, pltpu.roll(share, 1, 1))
    scale = -1.0 / implicit_ratio
    total = total + jnp.where(row == 0, scale * end_products[0], 0.0)
    total = total + jnp.where(row == rows - 1, scale * end_products[1], 0.0)
    sensitivity[...] = total * (0.5 / conduct)


def in_hbm(x):
    return pltpu.with_memory_space_constraint(x, pltpu.HBM)


def f32(*shape):
    return jax.ShapeDtypeStruct(shape, jnp.float32)


VMEM = pl.BlockSpec(memory_space=pltpu.VMEM)
PARAMS = pltpu.CompilerParams(vmem_limit_bytes=40 * 1024 * 1024)


def per_device(head_before, log_conductivity, fixed_mask, well_cells, pump_rates, adjoint_seed):
    tests, rows, columns = head_before.shape
    tiles = columns // LANES
    devices = lax.axis_size("gx")
    peers = lax.axis_size("gy")
    hb = head_before.reshape(tests * rows, columns)
    seed = adjoint_seed.reshape(tests * rows, columns)

    side = f32(rows, LANES)
    part = f32(tiles * tests * rows, LANES)
    out_rows = 2 * tests + 3
    back_rows = 2 * tests + 2

    def exchanged(rows_of_all):
        flat = rows_of_all.reshape(devices, 1, rows_of_all.size // devices)
        return lax.all_to_all(flat, "gx", 0, 0).reshape(rows_of_all.shape)

    anywhere = pl.BlockSpec(memory_space=pl.ANY)
    message, heads_part, adjoint_part, first, last, to_right, to_left, own = pl.pallas_call(
        functools.partial(local_kernel, rows, tests, columns * peers),
        in_specs=[anywhere] * 6,
        out_specs=[anywhere] + [VMEM] * 7,
        out_shape=[f32(devices * out_rows, LANES), part, part] + [f32(rows, columns)] * 2 + [side] * 3,
        scratch_shapes=[pltpu.SMEM((tests,), jnp.int32), pltpu.SMEM((tests,), jnp.float32)]
        + [pltpu.VMEM((tests * rows, columns), jnp.float32)] * 2
        + [pltpu.VMEM((rows, columns), jnp.float32), pltpu.VMEM((rows, columns), jnp.int32)]
        + [pltpu.VMEM((devices * out_rows, LANES), jnp.float32)]
        + [pltpu.SemaphoreType.DMA((6,)), pltpu.SemaphoreType.DMA]
        + [pltpu.VMEM((tiles * tests * rows, LANES), jnp.float32)] * 2
        + [pltpu.VMEM((rows * tiles, LANES), jnp.float32)] * 7,
        compiler_params=PARAMS,
        name="local",
    )(*[in_hbm(x) for x in (well_cells, pump_rates, hb, seed, log_conductivity, fixed_mask)])
    got = exchanged(message)
    from_right = lax.ppermute(to_left, "gy", [(i + 1, i) for i in range(peers - 1)])
    from_left = lax.ppermute(to_right, "gy", [(i, i + 1) for i in range(peers - 1)])
    reply, side_part, side_first, side_last = pl.pallas_call(
        functools.partial(line_kernel, devices, rows, tests),
        in_specs=[VMEM] * 4,
        out_specs=[VMEM] * 4,
        out_shape=[f32(devices * back_rows, LANES)] + [side] * 3,
        compiler_params=PARAMS,
        name="line",
    )(got, from_left, from_right, own)
    answer = exchanged(reply)
    heads, sensitivity = pl.pallas_call(
        functools.partial(final_kernel, rows, tests),
        in_specs=[VMEM] * 12,
        out_specs=[VMEM] * 2,
        out_shape=[f32(tests * rows, columns), f32(rows, columns)],
        scratch_shapes=[pltpu.VMEM((devices + SUBLANES, LANES), jnp.float32)],
        compiler_params=PARAMS,
        name="final",
    )(
        hb, log_conductivity, heads_part, adjoint_part, first, last, answer, from_left, from_right,
        side_part, side_first, side_last,
    )
    return heads.reshape(tests, rows, columns), sensitivity


def solution(mesh):
    return jax.shard_map(
        per_device,
        mesh=mesh,
        in_specs=(P(None, "gx", "gy"), P("gx", "gy"), P("gx", "gy"), P(), P(), P(None, "gx", "gy")),
        out_specs=(P(None, "gx", "gy"), P("gx", "gy")),
        check_vma=False,
    )
```

```python
import functools

import jax
import jax.numpy as jnp
from jax import lax
from jax.experimental import pallas as pl
from jax.experimental.pallas import tpu as pltpu
from jax.sharding import PartitionSpec as P

implicit_ratio = 4000.0
explicit_ratio = 0.1
LANES = 128
SUBLANES = 8


def spread_columns(lane, pieces):
    out = jnp.zeros(lane.shape, jnp.float32)
    for low, count, column in pieces:
        out = jnp.where((lane >= low) & (lane < low + count), column, out)
    return out


def edge_messages(rows, tests, hb, seed, conduct, active, to_right, to_left, own):
    columns = hb.shape[1]
    lane = lax.broadcasted_iota(jnp.int32, (rows, LANES), 1)
    sides = []
    for c in (0, columns - 1):
        column = slice(c, c + 1)
        heads = [hb[rows * t : rows * (t + 1), column] for t in range(tests)]
        seeds = [active[:, column] * seed[rows * t : rows * (t + 1), column] for t in range(tests)]
        sides.append((conduct[:, column], active[:, column], heads, seeds))

    def packed(side, odd, with_seed):
        conduct, active, heads, seeds = sides[side]
        base = tests * odd
        pieces = [(2 * tests + base + t, 1, heads[t]) for t in range(tests)]
        pieces += [(4 * tests + base, tests, conduct), (6 * tests + base, tests, active)]
        if with_seed:
            pieces += [(base + t, 1, seeds[t]) for t in range(tests)]
        return spread_columns(lane, pieces)

    to_right[...] = packed(1, 0, True)
    to_left[...] = packed(0, 1, True)
    own[...] = packed(0, 0, False) + packed(1, 1, False)


def eliminate(conduct, active):
    rows = len(conduct)
    faces = [
        (2.0 * implicit_ratio) * conduct[i] * conduct[i + 1] / (conduct[i] + conduct[i + 1]) for i in range(rows - 1)
    ]
    below = [None] + [active[i] * faces[i - 1] for i in range(1, rows)]
    above = [active[i] * faces[i] for i in range(rows - 1)] + [None]
    scales, products, inverses = [], [], []
    for i in range(rows):
        diagonal = 1.0 + (above[i] if i == 0 else below[i] if i == rows - 1 else below[i] + above[i])
        scales.append(1.0 / diagonal)
    excess = scales[0]
    products.append(jnp.ones_like(excess))
    for i in range(1, rows):
        excess = scales[i] * products[-1] + (scales[i] * below[i]) * excess
        products.append(excess if i == rows - 1 else excess + (scales[i] * above[i]) * products[-1])
    inverses = [scales[0]] + [scales[i] * products[i - 1] / products[i] for i in range(1, rows)]
    gains = [None] + [below[i] * inverses[i - 1] for i in range(1, rows)]
    backs = [above[i] * inverses[i] for i in range(rows - 1)] + [None]
    return gains, inverses, backs


def sweep(gains, inverses, backs, right):
    rows = len(right)
    held = [right[0]]
    for i in range(1, rows):
        held.append(right[i] + gains[i] * held[-1])
    values = [None] * rows
    values[-1] = held[-1] * inverses[-1]
    for i in range(rows - 2, -1, -1):
        values[i] = held[i] * inverses[i] + backs[i] * values[i + 1]
    return values


def responses(gains, inverses, backs, active):
    rows = len(active)
    held = [active[0]]
    for i in range(1, rows):
        held.append(gains[i] * held[-1])
    first, last = [None] * rows, [None] * rows
    first[-1] = held[-1] * inverses[-1]
    last[-1] = active[-1] * inverses[-1]
    for i in range(rows - 2, -1, -1):
        first[i] = held[i] * inverses[i] + backs[i] * first[i + 1]
        last[i] = backs[i] * last[i + 1]
    return first, last


def local_kernel(
    rows, tests, total_columns, wells_all, rates_all, hb_all, seed_all, logk_all, mask_all,
    message_all, heads_part, adjoint_part, first_out, last_out, to_right, to_left, own,
    wells, rates, hb, seed, logk, mask, message, arrived, sent,
    right, weighed, cond_c, act_c, gain_c, inv_c, back_c, first_c, last_c,
):
    pairs = (
        (logk_all, logk), (mask_all, mask), (hb_all, hb), (seed_all, seed), (wells_all, wells), (rates_all, rates),
    )
    copies = [pltpu.make_async_copy(whole, here, arrived.at[n]) for n, (whole, here) in enumerate(pairs)]
    for copy in copies:
        copy.start()
    columns = hb.shape[1]
    tiles = columns // LANES
    field = tests * rows
    for copy in copies:
        copy.wait()
    conduct = jnp.exp(logk[...])
    active = (1 - mask[...]).astype(jnp.float32)
    for k in range(tiles):
        cond_c[pl.ds(k, rows, stride=tiles), :] = conduct[:, k * LANES : (k + 1) * LANES]
        act_c[pl.ds(k, rows, stride=tiles), :] = active[:, k * LANES : (k + 1) * LANES]
    cond_rows = [cond_c[tiles * i : tiles * (i + 1), :] for i in range(rows)]
    act_rows = [act_c[tiles * i : tiles * (i + 1), :] for i in range(rows)]
    gains, inverses, backs = eliminate(cond_rows, act_rows)
    first, last = responses(gains, inverses, backs, act_rows)
    for i in range(rows):
        here = slice(tiles * i, tiles * (i + 1))
        if i > 0:
            gain_c[here, :] = gains[i]
        inv_c[here, :] = inverses[i]
        if i < rows - 1:
            back_c[here, :] = backs[i]
        first_c[here, :] = first[i]
        last_c[here, :] = last[i]
    half = 0.5 / implicit_ratio
    first_end = first[0] + half / cond_rows[0]
    last_end = last[-1] + half / cond_rows[-1]
    across = first[-1]

    lane = lax.broadcasted_iota(jnp.int32, (rows, columns), 1)
    cond_north = pltpu.roll(conduct, columns - 1, 1)
    face = (2.0 * explicit_ratio) * conduct * cond_north / (conduct + cond_north)
    face = jnp.where(lane == columns - 1, 0.0, face)
    for t in range(tests):
        here = slice(rows * t, rows * (t + 1))
        head = hb[here, :]
        flow = face * (pltpu.roll(head, columns - 1, 1) - head)
        value = head + active * (flow - pltpu.roll(flow, 1, 1))
        seeded = active * seed[here, :]
        for k in range(tiles):
            lanes = slice(k * LANES, (k + 1) * LANES)
            there = slice(k * field + rows * t, k * field + rows * (t + 1))
            right[there, :] = value[:, lanes]
            weighed[there, :] = seeded[:, lanes]
    row_start = lax.axis_index("gx") * rows
    column_start = lax.axis_index("gy") * columns
    row_lane = lax.broadcasted_iota(jnp.int32, (1, LANES), 1)
    shift = total_columns.bit_length() - 1
    places = []
    for t in range(tests):
        if total_columns == 1 << shift:
            well_row = lax.shift_right_logical(wells[t], shift)
        else:
            well_row = wells[t] // total_columns
        well_column = wells[t] - well_row * total_columns - column_start
        well_row = well_row - row_start
        inside = (well_row >= 0) & (well_row < rows) & (well_column >= 0) & (well_column < columns)
        places.append((inside, well_row, well_column))

    @pl.when(functools.reduce(jnp.logical_or, [inside for inside, _, _ in places]))
    def _():
        for t, (inside, well_row, well_column) in enumerate(places):

            @pl.when(inside)
            def _():
                tile = well_column // LANES
                act_row = act_c[pl.ds(tiles * well_row + tile, 1), :]
                there = pl.ds(tile * field + rows * t + well_row, 1)
                added = jnp.where(row_lane == well_column % LANES, act_row * rates[t], 0.0)
                right[there, :] = right[there, :] + added

    for k in range(tiles):
        lanes = slice(k * LANES, (k + 1) * LANES)
        gain_k = [None] + [gain_c[tiles * i + k : tiles * i + k + 1, :] for i in range(1, rows)]
        inv_k = [inv_c[tiles * i + k : tiles * i + k + 1, :] for i in range(rows)]
        back_k = [back_c[tiles * i + k : tiles * i + k + 1, :] for i in range(rows - 1)] + [None]
        for core, (source, out) in enumerate(((right, heads_part), (weighed, adjoint_part))):
            given = [source[pl.ds(k * field + i, tests, stride=rows), :] for i in range(rows)]
            values = sweep(gain_k, inv_k, back_k, given)
            for i in range(rows):
                start = k * field + i * tests
                out[start : start + tests, :] = values[i]
            start = (2 * k + core) * (2 * tests + 3)
            message[start : start + tests, :] = values[0]
            message[start + tests : start + 2 * tests, :] = values[-1]
            for r, value in enumerate((first_end, last_end, across)):
                message[start + 2 * tests + r : start + 2 * tests + r + 1, :] = value[k : k + 1, :]
        first_out[:, lanes] = first_c[pl.ds(k, rows, stride=tiles), :]
        last_out[:, lanes] = last_c[pl.ds(k, rows, stride=tiles), :]
    sending = pltpu.make_async_copy(message, message_all, sent)
    sending.start()
    edge_messages(rows, tests, hb, seed, conduct, active, to_right, to_left, own)
    sending.wait()


def chain(first_end, last_end, across, first_value, last_value):
    count = len(first_end)
    diag = [None] + [last_end[i - 1] + first_end[i] for i in range(1, count)]
    load = [None] + [last_value[i - 1] - first_value[i] for i in range(1, count)]
    middle = count // 2
    inverse = [None] * count
    reciprocal = [None] + [1.0 / diag[i] for i in range(1, count)]
    loss = [None] + [(across[i] * reciprocal[i]) * (across[i] * reciprocal[i + 1]) for i in range(1, count - 1)]
    for order in (range(1, middle), range(count - 1, middle, -1)):
        before = last = jnp.ones_like(diag[1])
        previous = None
        for i in order:
            if previous is not None:
                before, last = last, last - loss[min(i, previous)] * before
            inverse[i] = reciprocal[i] if previous is None else reciprocal[i] * before / last
            if previous is not None:
                load[i] = load[i] + (across[min(i, previous)] * inverse[previous]) * load[previous]
            previous = i
    below = across[middle - 1] * inverse[middle - 1]
    above = across[middle] * inverse[middle + 1]
    diag[middle] = diag[middle] - below * across[middle - 1] - above * across[middle]
    load[middle] = load[middle] + below * load[middle - 1] + above * load[middle + 1]
    flux = [None] * count
    flux[middle] = load[middle] / diag[middle]
    for i in range(middle - 1, 0, -1):
        flux[i] = (load[i] + across[i] * flux[i + 1]) * inverse[i]
    for i in range(middle + 1, count):
        flux[i] = (load[i] + across[i - 1] * flux[i - 1]) * inverse[i]
    nothing = jnp.zeros_like(flux[middle])
    return [nothing] + flux[1:] + [nothing]


def side_lanes(rows, tests, from_left, from_right, own, side_part, side_first, side_last):
    halo = from_left[...] + from_right[...]
    mine = own[...]
    side_lane = lax.broadcasted_iota(jnp.int32, (rows, LANES), 1)
    outer = side_lane < 2 * tests
    halo_k = pltpu.roll(halo, LANES - 2 * tests, 1)
    own_k = pltpu.roll(mine, LANES - 2 * tests, 1)
    cond_s = jnp.where(outer, pltpu.roll(halo, LANES - 4 * tests, 1), own_k)
    cond_s = jnp.where(cond_s > 0.0, cond_s, 1.0)
    act_s = jnp.where(outer, pltpu.roll(halo, LANES - 6 * tests, 1), pltpu.roll(mine, LANES - 4 * tests, 1))
    side_face = (2.0 * explicit_ratio) * cond_s * halo_k / (cond_s + halo_k)
    given_s = jnp.where(outer, halo, act_s * side_face * (halo - mine))
    cond_sr = [cond_s[i : i + 1, :] for i in range(rows)]
    act_sr = [act_s[i : i + 1, :] for i in range(rows)]
    gains_s, inv_s, backs_s = eliminate(cond_sr, act_sr)
    first_s, last_s = responses(gains_s, inv_s, backs_s, act_sr)
    part_s = sweep(gains_s, inv_s, backs_s, [given_s[i : i + 1, :] for i in range(rows)])
    for i in range(rows):
        side_part[i : i + 1, :] = part_s[i]
        side_first[i : i + 1, :] = first_s[i]
        side_last[i : i + 1, :] = last_s[i]
    half = 0.5 / implicit_ratio
    ends = (
        part_s[0], part_s[-1], first_s[0] + half / cond_sr[0], last_s[-1] + half / cond_sr[-1], first_s[-1],
    )
    return ends


def line_kernel(devices, rows, tests, got, from_left, from_right, own, reply, side_part, side_first, side_last):
    out_rows, back_rows = 2 * tests + 3, 2 * tests + 2

    def pick(low, high):
        return [got[out_rows * d + low : out_rows * d + high, :] for d in range(devices)]

    ends = [pick(2 * tests + r, 2 * tests + r + 1) for r in range(3)]
    flux = chain(*ends, pick(0, tests), pick(tests, 2 * tests))
    side = side_lanes(rows, tests, from_left, from_right, own, side_part, side_first, side_last)
    width = 4 * tests
    lane = lax.broadcasted_iota(jnp.int32, (1, LANES), 1)
    joined = side[0]
    for r in range(1, 4):
        joined = jnp.where(lane >= width * r, pltpu.roll(side[r], width * r, 1), joined)
    for d in range(devices):
        start = back_rows * d
        reply[start : start + tests, :] = flux[d]
        reply[start + tests : start + 2 * tests, :] = flux[d + 1]
        reply[start + 2 * tests : start + 2 * tests + 1, :] = joined
        reply[start + 2 * tests + 1 : start + back_rows, :] = side[4]


def final_kernel(
    rows, tests, hb, logk, heads_part, adjoint_part, first_in, last_in, got, from_left, from_right,
    side_part, side_first, side_last, heads, sensitivity, held,
):
    columns = hb.shape[1]
    tiles = columns // LANES
    back_rows = 2 * tests + 2
    devices = got.shape[0] // back_rows
    width = 4 * tests

    def sent_row(r):
        return jnp.concatenate([got[back_rows * d + r : back_rows * d + r + 1, :] for d in range(devices)], axis=0)

    packed = sent_row(2 * tests)
    ends = [packed] + [pltpu.roll(packed, LANES - width * r, 1) for r in range(1, 4)] + [sent_row(2 * tests + 1)]
    ends = [[value[d : d + 1, :] for d in range(devices)] for value in ends]
    for d, value in enumerate(chain(ends[2], ends[3], ends[4], ends[0], ends[1])):
        held[d : d + 1, :] = value
    me = lax.axis_index("gx")
    side_flux = [held[pl.ds(me, 1), :], held[pl.ds(me + 1, 1), :]]
    side = side_part[...] + side_first[...] * side_flux[0] - side_last[...] * side_flux[1]
    halo = from_left[...] + from_right[...]
    conduct = jnp.exp(logk[...])
    first = first_in[...]
    last = last_in[...]
    lane = lax.broadcasted_iota(jnp.int32, (rows, columns), 1)
    row = lax.broadcasted_iota(jnp.int32, (rows, columns), 0)
    at_start = lane == 0
    at_end = lane == columns - 1

    def wide(core, r):
        starts = [back_rows * (2 * k + core) for k in range(tiles)]
        return jnp.concatenate([got[starts[k] + r : starts[k] + r + 1, :] for k in range(tiles)], axis=1)

    def joined(part, t):
        starts = [k * tests * rows + t for k in range(tiles)]
        return jnp.concatenate([part[pl.ds(start, rows, stride=tests), :] for start in starts], axis=1)

    def beside(values, index):
        return values[:, index : index + 1]

    row_lane = lax.broadcasted_iota(jnp.int32, (1, columns), 1)
    end_products = [jnp.zeros((1, columns), jnp.float32)] * 2
    along_rows = jnp.zeros((rows, columns), jnp.float32)
    along_columns = jnp.zeros((rows, columns), jnp.float32)
    start_face = jnp.zeros((rows, LANES), jnp.float32)
    for t in range(tests):
        here = slice(rows * t, rows * (t + 1))
        fluxes = [[wide(core, base + t) for base in (0, tests)] for core in (0, 1)]
        head = joined(heads_part, t) + first * fluxes[0][0] - last * fluxes[0][1]
        head = head + jnp.where(at_start, beside(side, 2 * tests + t), 0.0)
        head = head + jnp.where(at_end, beside(side, 3 * tests + t), 0.0)
        heads[here, :] = head
        weight = joined(adjoint_part, t) + first * fluxes[1][0] - last * fluxes[1][1]
        for end in (0, 1):
            side_row = side_flux[end]
            whole = fluxes[0][end] + jnp.where(row_lane == 0, beside(side_row, 2 * tests + t), 0.0)
            whole = whole + jnp.where(row_lane == columns - 1, beside(side_row, 3 * tests + t), 0.0)
            end_products[end] = end_products[end] + whole * fluxes[1][end]
        east_head = pltpu.roll(head, rows - 1, 0)
        east_weight = pltpu.roll(weight, rows - 1, 0)
        along_rows = along_rows + (east_head - head) * (weight - east_weight)
        old = hb[here, :]
        north_old = jnp.where(at_end, beside(halo, 3 * tests + t), pltpu.roll(old, columns - 1, 1))
        north_weight = jnp.where(at_end, beside(side, tests + t), pltpu.roll(weight, columns - 1, 1))
        along_columns = along_columns + (north_old - old) * (weight - north_weight)
        start_face = start_face + (old[:, :LANES] - beside(halo, 2 * tests + t)) * (
            beside(side, t) - weight[:, :LANES]
        )
    cond_east = pltpu.roll(conduct, rows - 1, 0)
    face = 2.0 * conduct * cond_east / (conduct + cond_east)
    face = jnp.where(row == rows - 1, 0.0, face)
    share = implicit_ratio * face * face * along_rows
    total = share + pltpu.roll(share, 1, 0)
    cond_north = jnp.where(at_end, beside(halo, 5 * tests), pltpu.roll(conduct, columns - 1, 1))
    face = 2.0 * conduct * cond_north / (conduct + cond_north)
    share = explicit_ratio * face * face * along_columns
    cond_start = conduct[:, :LANES]
    cond_south = jnp.broadcast_to(beside(halo, 4 * tests), (rows, LANES))
    face = 2.0 * cond_start * cond_south / (cond_start + cond_south)
    start_share = explicit_ratio * face * face * start_face
    start_share = jnp.concatenate([start_share, jnp.zeros((rows, columns - LANES), jnp.float32)], axis=1)
    total = total + share + jnp.where(at_start, start_share, pltpu.roll(share, 1, 1))
    scale = -1.0 / implicit_ratio
    total = total + jnp.where(row == 0, scale * end_products[0], 0.0)
    total = total + jnp.where(row == rows - 1, scale * end_products[1], 0.0)
    sensitivity[...] = total * (0.5 / conduct)


def in_hbm(x):
    return pltpu.with_memory_space_constraint(x, pltpu.HBM)


def f32(*shape):
    return jax.ShapeDtypeStruct(shape, jnp.float32)


VMEM = pl.BlockSpec(memory_space=pltpu.VMEM)
PARAMS = pltpu.CompilerParams(vmem_limit_bytes=40 * 1024 * 1024)


def per_device(head_before, log_conductivity, fixed_mask, well_cells, pump_rates, adjoint_seed):
    tests, rows, columns = head_before.shape
    tiles = columns // LANES
    devices = lax.axis_size("gx")
    peers = lax.axis_size("gy")
    hb = head_before.reshape(tests * rows, columns)
    seed = adjoint_seed.reshape(tests * rows, columns)

    side = f32(rows, LANES)
    part = f32(tiles * tests * rows, LANES)
    out_rows = 2 * tests + 3
    back_rows = 2 * tests + 2

    def exchanged(rows_of_all):
        flat = rows_of_all.reshape(devices, 1, rows_of_all.size // devices)
        return lax.all_to_all(flat, "gx", 0, 0).reshape(rows_of_all.shape)

    anywhere = pl.BlockSpec(memory_space=pl.ANY)
    message, heads_part, adjoint_part, first, last, to_right, to_left, own = pl.pallas_call(
        functools.partial(local_kernel, rows, tests, columns * peers),
        in_specs=[anywhere] * 6,
        out_specs=[anywhere] + [VMEM] * 7,
        out_shape=[f32(devices * out_rows, LANES), part, part] + [f32(rows, columns)] * 2 + [side] * 3,
        scratch_shapes=[pltpu.SMEM((tests,), jnp.int32), pltpu.SMEM((tests,), jnp.float32)]
        + [pltpu.VMEM((tests * rows, columns), jnp.float32)] * 2
        + [pltpu.VMEM((rows, columns), jnp.float32), pltpu.VMEM((rows, columns), jnp.int32)]
        + [pltpu.VMEM((devices * out_rows, LANES), jnp.float32)]
        + [pltpu.SemaphoreType.DMA((6,)), pltpu.SemaphoreType.DMA]
        + [pltpu.VMEM((tiles * tests * rows, LANES), jnp.float32)] * 2
        + [pltpu.VMEM((rows * tiles, LANES), jnp.float32)] * 7,
        compiler_params=PARAMS,
        name="local",
    )(*[in_hbm(x) for x in (well_cells, pump_rates, hb, seed, log_conductivity, fixed_mask)])
    got = exchanged(message)
    from_right = lax.ppermute(to_left, "gy", [(i + 1, i) for i in range(peers - 1)])
    from_left = lax.ppermute(to_right, "gy", [(i, i + 1) for i in range(peers - 1)])
    reply, side_part, side_first, side_last = pl.pallas_call(
        functools.partial(line_kernel, devices, rows, tests),
        in_specs=[VMEM] * 4,
        out_specs=[VMEM] * 4,
        out_shape=[f32(devices * back_rows, LANES)] + [side] * 3,
        compiler_params=PARAMS,
        name="line",
    )(got, from_left, from_right, own)
    answer = exchanged(reply)
    heads, sensitivity = pl.pallas_call(
        functools.partial(final_kernel, rows, tests),
        in_specs=[VMEM] * 12,
        out_specs=[VMEM] * 2,
        out_shape=[f32(tests * rows, columns), f32(rows, columns)],
        scratch_shapes=[pltpu.VMEM((devices + SUBLANES, LANES), jnp.float32)],
        compiler_params=PARAMS,
        name="final",
    )(
        hb, log_conductivity, heads_part, adjoint_part, first, last, answer, from_left, from_right,
        side_part, side_first, side_last,
    )
    return heads.reshape(tests, rows, columns), sensitivity


def solution(mesh):
    return jax.shard_map(
        per_device,
        mesh=mesh,
        in_specs=(P(None, "gx", "gy"), P("gx", "gy"), P("gx", "gy"), P(), P(), P(None, "gx", "gy")),
        out_specs=(P(None, "gx", "gy"), P("gx", "gy")),
        check_vma=False,
    )
```

```python
import functools

import jax
import jax.numpy as jnp
from jax import lax
from jax.experimental import pallas as pl
from jax.experimental.pallas import tpu as pltpu
from jax.sharding import PartitionSpec as P

implicit_ratio = 4000.0
explicit_ratio = 0.1
LANES = 128
SUBLANES = 8


def spread_columns(lane, pieces):
    out = jnp.zeros(lane.shape, jnp.float32)
    for low, count, column in pieces:
        out = jnp.where((lane >= low) & (lane < low + count), column, out)
    return out


def edge_messages(rows, tests, hb, seed, conduct, active, to_right, to_left, own):
    columns = hb.shape[1]
    lane = lax.broadcasted_iota(jnp.int32, (rows, LANES), 1)
    sides = []
    for c in (0, columns - 1):
        column = slice(c, c + 1)
        heads = [hb[rows * t : rows * (t + 1), column] for t in range(tests)]
        seeds = [active[:, column] * seed[rows * t : rows * (t + 1), column] for t in range(tests)]
        sides.append((conduct[:, column], active[:, column], heads, seeds))

    def packed(side, odd, with_seed):
        conduct, active, heads, seeds = sides[side]
        base = tests * odd
        pieces = [(2 * tests + base + t, 1, heads[t]) for t in range(tests)]
        pieces += [(4 * tests + base, tests, conduct), (6 * tests + base, tests, active)]
        if with_seed:
            pieces += [(base + t, 1, seeds[t]) for t in range(tests)]
        return spread_columns(lane, pieces)

    to_right[...] = packed(1, 0, True)
    to_left[...] = packed(0, 1, True)
    own[...] = packed(0, 0, False) + packed(1, 1, False)


def eliminate(conduct, active):
    rows = len(conduct)
    faces = [
        (2.0 * implicit_ratio) * conduct[i] * conduct[i + 1] / (conduct[i] + conduct[i + 1]) for i in range(rows - 1)
    ]
    below = [None] + [active[i] * faces[i - 1] for i in range(1, rows)]
    above = [active[i] * faces[i] for i in range(rows - 1)] + [None]
    scales, products, inverses = [], [], []
    for i in range(rows):
        diagonal = 1.0 + (above[i] if i == 0 else below[i] if i == rows - 1 else below[i] + above[i])
        scales.append(1.0 / diagonal)
    excess = scales[0]
    products.append(jnp.ones_like(excess))
    for i in range(1, rows):
        excess = scales[i] * products[-1] + (scales[i] * below[i]) * excess
        products.append(excess if i == rows - 1 else excess + (scales[i] * above[i]) * products[-1])
    inverses = [scales[0]] + [scales[i] * products[i - 1] / products[i] for i in range(1, rows)]
    gains = [None] + [below[i] * inverses[i - 1] for i in range(1, rows)]
    backs = [above[i] * inverses[i] for i in range(rows - 1)] + [None]
    return gains, inverses, backs


def sweep(gains, inverses, backs, right):
    rows = len(right)
    held = [right[0]]
    for i in range(1, rows):
        held.append(right[i] + gains[i] * held[-1])
    values = [None] * rows
    values[-1] = held[-1] * inverses[-1]
    for i in range(rows - 2, -1, -1):
        values[i] = held[i] * inverses[i] + backs[i] * values[i + 1]
    return values


def responses(gains, inverses, backs, active):
    rows = len(active)
    held = [active[0]]
    for i in range(1, rows):
        held.append(gains[i] * held[-1])
    first, last = [None] * rows, [None] * rows
    first[-1] = held[-1] * inverses[-1]
    last[-1] = active[-1] * inverses[-1]
    for i in range(rows - 2, -1, -1):
        first[i] = held[i] * inverses[i] + backs[i] * first[i + 1]
        last[i] = backs[i] * last[i + 1]
    return first, last


def local_kernel(
    rows, tests, total_columns, wells_all, rates_all, hb_all, seed_all, logk_all, mask_all,
    message_all, heads_part, adjoint_part, first_out, last_out, to_right, to_left, own,
    wells, rates, hb, seed, logk, mask, message, arrived, sent,
    right, weighed, cond_c, act_c, gain_c, inv_c, back_c, first_c, last_c,
):
    pairs = (
        (logk_all, logk), (mask_all, mask), (hb_all, hb), (seed_all, seed), (wells_all, wells), (rates_all, rates),
    )
    copies = [pltpu.make_async_copy(whole, here, arrived.at[n]) for n, (whole, here) in enumerate(pairs)]
    for copy in copies:
        copy.start()
    columns = hb.shape[1]
    tiles = columns // LANES
    field = tests * rows
    for copy in copies:
        copy.wait()
    conduct = jnp.exp(logk[...])
    active = (1 - mask[...]).astype(jnp.float32)
    for k in range(tiles):
        cond_c[pl.ds(k, rows, stride=tiles), :] = conduct[:, k * LANES : (k + 1) * LANES]
        act_c[pl.ds(k, rows, stride=tiles), :] = active[:, k * LANES : (k + 1) * LANES]
    cond_rows = [cond_c[tiles * i : tiles * (i + 1), :] for i in range(rows)]
    act_rows = [act_c[tiles * i : tiles * (i + 1), :] for i in range(rows)]
    gains, inverses, backs = eliminate(cond_rows, act_rows)
    first, last = responses(gains, inverses, backs, act_rows)
    for i in range(rows):
        here = slice(tiles * i, tiles * (i + 1))
        if i > 0:
            gain_c[here, :] = gains[i]
        inv_c[here, :] = inverses[i]
        if i < rows - 1:
            back_c[here, :] = backs[i]
        first_c[here, :] = first[i]
        last_c[here, :] = last[i]
    half = 0.5 / implicit_ratio
    first_end = first[0] + half / cond_rows[0]
    last_end = last[-1] + half / cond_rows[-1]
    across = first[-1]

    lane = lax.broadcasted_iota(jnp.int32, (rows, columns), 1)
    cond_north = pltpu.roll(conduct, columns - 1, 1)
    face = (2.0 * explicit_ratio) * conduct * cond_north / (conduct + cond_north)
    face = jnp.where(lane == columns - 1, 0.0, face)
    for t in range(tests):
        here = slice(rows * t, rows * (t + 1))
        head = hb[here, :]
        flow = face * (pltpu.roll(head, columns - 1, 1) - head)
        value = head + active * (flow - pltpu.roll(flow, 1, 1))
        seeded = active * seed[here, :]
        for k in range(tiles):
            lanes = slice(k * LANES, (k + 1) * LANES)
            there = slice(k * field + rows * t, k * field + rows * (t + 1))
            right[there, :] = value[:, lanes]
            weighed[there, :] = seeded[:, lanes]
    row_start = lax.axis_index("gx") * rows
    column_start = lax.axis_index("gy") * columns
    row_lane = lax.broadcasted_iota(jnp.int32, (1, LANES), 1)
    shift = total_columns.bit_length() - 1
    places = []
    for t in range(tests):
        if total_columns == 1 << shift:
            well_row = lax.shift_right_logical(wells[t], shift)
        else:
            well_row = wells[t] // total_columns
        well_column = wells[t] - well_row * total_columns - column_start
        well_row = well_row - row_start
        inside = (well_row >= 0) & (well_row < rows) & (well_column >= 0) & (well_column < columns)
        places.append((inside, well_row, well_column))

    @pl.when(functools.reduce(jnp.logical_or, [inside for inside, _, _ in places]))
    def _():
        for t, (inside, well_row, well_column) in enumerate(places):

            @pl.when(inside)
            def _():
                tile = well_column // LANES
                act_row = act_c[pl.ds(tiles * well_row + tile, 1), :]
                there = pl.ds(tile * field + rows * t + well_row, 1)
                added = jnp.where(row_lane == well_column % LANES, act_row * rates[t], 0.0)
                right[there, :] = right[there, :] + added

    for k in range(tiles):
        lanes = slice(k * LANES, (k + 1) * LANES)
        gain_k = [None] + [gain_c[tiles * i + k : tiles * i + k + 1, :] for i in range(1, rows)]
        inv_k = [inv_c[tiles * i + k : tiles * i + k + 1, :] for i in range(rows)]
        back_k = [back_c[tiles * i + k : tiles * i + k + 1, :] for i in range(rows - 1)] + [None]
        for core, (source, out) in enumerate(((right, heads_part), (weighed, adjoint_part))):
            given = [source[pl.ds(k * field + i, tests, stride=rows), :] for i in range(rows)]
            values = sweep(gain_k, inv_k, back_k, given)
            for i in range(rows):
                start = k * field + i * tests
                out[start : start + tests, :] = values[i]
            start = (2 * k + core) * (2 * tests + 3)
            message[start : start + tests, :] = values[0]
            message[start + tests : start + 2 * tests, :] = values[-1]
            for r, value in enumerate((first_end, last_end, across)):
                message[start + 2 * tests + r : start + 2 * tests + r + 1, :] = value[k : k + 1, :]
        first_out[:, lanes] = first_c[pl.ds(k, rows, stride=tiles), :]
        last_out[:, lanes] = last_c[pl.ds(k, rows, stride=tiles), :]
    sending = pltpu.make_async_copy(message, message_all, sent)
    sending.start()
    edge_messages(rows, tests, hb, seed, conduct, active, to_right, to_left, own)
    sending.wait()


def chain(first_end, last_end, across, first_value, last_value):
    count = len(first_end)
    diag = [None] + [last_end[i - 1] + first_end[i] for i in range(1, count)]
    load = [None] + [last_value[i - 1] - first_value[i] for i in range(1, count)]
    middle = count // 2
    inverse = [None] * count
    reciprocal = [None] + [1.0 / diag[i] for i in range(1, count)]
    loss = [None] + [(across[i] * reciprocal[i]) * (across[i] * reciprocal[i + 1]) for i in range(1, count - 1)]
    for order in (range(1, middle), range(count - 1, middle, -1)):
        before = last = jnp.ones_like(diag[1])
        previous = None
        for i in order:
            if previous is not None:
                before, last = last, last - loss[min(i, previous)] * before
            inverse[i] = reciprocal[i] if previous is None else reciprocal[i] * before / last
            if previous is not None:
                load[i] = load[i] + (across[min(i, previous)] * inverse[previous]) * load[previous]
            previous = i
    below = across[middle - 1] * inverse[middle - 1]
    above = across[middle] * inverse[middle + 1]
    diag[middle] = diag[middle] - below * across[middle - 1] - above * across[middle]
    load[middle] = load[middle] + below * load[middle - 1] + above * load[middle + 1]
    flux = [None] * count
    flux[middle] = load[middle] / diag[middle]
    for i in range(middle - 1, 0, -1):
        flux[i] = (load[i] + across[i] * flux[i + 1]) * inverse[i]
    for i in range(middle + 1, count):
        flux[i] = (load[i] + across[i - 1] * flux[i - 1]) * inverse[i]
    nothing = jnp.zeros_like(flux[middle])
    return [nothing] + flux[1:] + [nothing]


def side_lanes(rows, tests, from_left, from_right, own, side_part, side_first, side_last):
    halo = from_left[...] + from_right[...]
    mine = own[...]
    side_lane = lax.broadcasted_iota(jnp.int32, (rows, LANES), 1)
    outer = side_lane < 2 * tests
    halo_k = pltpu.roll(halo, LANES - 2 * tests, 1)
    own_k = pltpu.roll(mine, LANES - 2 * tests, 1)
    cond_s = jnp.where(outer, pltpu.roll(halo, LANES - 4 * tests, 1), own_k)
    cond_s = jnp.where(cond_s > 0.0, cond_s, 1.0)
    act_s = jnp.where(outer, pltpu.roll(halo, LANES - 6 * tests, 1), pltpu.roll(mine, LANES - 4 * tests, 1))
    side_face = (2.0 * explicit_ratio) * cond_s * halo_k / (cond_s + halo_k)
    given_s = jnp.where(outer, halo, act_s * side_face * (halo - mine))
    cond_sr = [cond_s[i : i + 1, :] for i in range(rows)]
    act_sr = [act_s[i : i + 1, :] for i in range(rows)]
    gains_s, inv_s, backs_s = eliminate(cond_sr, act_sr)
    first_s, last_s = responses(gains_s, inv_s, backs_s, act_sr)
    part_s = sweep(gains_s, inv_s, backs_s, [given_s[i : i + 1, :] for i in range(rows)])
    for i in range(rows):
        side_part[i : i + 1, :] = part_s[i]
        side_first[i : i + 1, :] = first_s[i]
        side_last[i : i + 1, :] = last_s[i]
    half = 0.5 / implicit_ratio
    ends = (
        part_s[0], part_s[-1], first_s[0] + half / cond_sr[0], last_s[-1] + half / cond_sr[-1], first_s[-1],
    )
    return ends


def keep_kernel(given, out):
    out[...] = given[...]


def side_kernel(rows, tests, from_left, from_right, own, side_part, side_first, side_last, side_rows):
    side = side_lanes(rows, tests, from_left, from_right, own, side_part, side_first, side_last)
    width = 4 * tests
    lane = lax.broadcasted_iota(jnp.int32, (1, LANES), 1)
    joined = side[0]
    for r in range(1, 4):
        joined = jnp.where(lane >= width * r, pltpu.roll(side[r], width * r, 1), joined)
    side_rows[0:1, :] = joined
    side_rows[1:2, :] = side[4]


def line_kernel(devices, tests, got, side_rows, reply):
    out_rows, back_rows = 2 * tests + 3, 2 * tests + 2

    def pick(low, high):
        return [got[out_rows * d + low : out_rows * d + high, :] for d in range(devices)]

    ends = [pick(2 * tests + r, 2 * tests + r + 1) for r in range(3)]
    flux = chain(*ends, pick(0, tests), pick(tests, 2 * tests))
    for d in range(devices):
        start = back_rows * d
        reply[start : start + tests, :] = flux[d]
        reply[start + tests : start + 2 * tests, :] = flux[d + 1]
        reply[start + 2 * tests : start + back_rows, :] = side_rows[0:2, :]


def final_kernel(
    rows, tests, hb, logk, heads_part, adjoint_part, first_in, last_in, got, from_left, from_right,
    side_part, side_first, side_last, heads, sensitivity, held,
):
    columns = hb.shape[1]
    tiles = columns // LANES
    back_rows = 2 * tests + 2
    devices = got.shape[0] // back_rows
    width = 4 * tests

    def sent_row(r):
        return jnp.concatenate([got[back_rows * d + r : back_rows * d + r + 1, :] for d in range(devices)], axis=0)

    packed = sent_row(2 * tests)
    ends = [packed] + [pltpu.roll(packed, LANES - width * r, 1) for r in range(1, 4)] + [sent_row(2 * tests + 1)]
    ends = [[value[d : d + 1, :] for d in range(devices)] for value in ends]
    for d, value in enumerate(chain(ends[2], ends[3], ends[4], ends[0], ends[1])):
        held[d : d + 1, :] = value
    me = lax.axis_index("gx")
    side_flux = [held[pl.ds(me, 1), :], held[pl.ds(me + 1, 1), :]]
    side = side_part[...] + side_first[...] * side_flux[0] - side_last[...] * side_flux[1]
    halo = from_left[...] + from_right[...]
    conduct = jnp.exp(logk[...])
    first = first_in[...]
    last = last_in[...]
    lane = lax.broadcasted_iota(jnp.int32, (rows, columns), 1)
    row = lax.broadcasted_iota(jnp.int32, (rows, columns), 0)
    at_start = lane == 0
    at_end = lane == columns - 1

    def wide(core, r):
        starts = [back_rows * (2 * k + core) for k in range(tiles)]
        return jnp.concatenate([got[starts[k] + r : starts[k] + r + 1, :] for k in range(tiles)], axis=1)

    def joined(part, t):
        starts = [k * tests * rows + t for k in range(tiles)]
        return jnp.concatenate([part[pl.ds(start, rows, stride=tests), :] for start in starts], axis=1)

    def beside(values, index):
        return values[:, index : index + 1]

    row_lane = lax.broadcasted_iota(jnp.int32, (1, columns), 1)
    end_products = [jnp.zeros((1, columns), jnp.float32)] * 2
    along_rows = jnp.zeros((rows, columns), jnp.float32)
    along_columns = jnp.zeros((rows, columns), jnp.float32)
    start_face = jnp.zeros((rows, LANES), jnp.float32)
    for t in range(tests):
        here = slice(rows * t, rows * (t + 1))
        fluxes = [[wide(core, base + t) for base in (0, tests)] for core in (0, 1)]
        head = joined(heads_part, t) + first * fluxes[0][0] - last * fluxes[0][1]
        head = head + jnp.where(at_start, beside(side, 2 * tests + t), 0.0)
        head = head + jnp.where(at_end, beside(side, 3 * tests + t), 0.0)
        heads[here, :] = head
        weight = joined(adjoint_part, t) + first * fluxes[1][0] - last * fluxes[1][1]
        for end in (0, 1):
            side_row = side_flux[end]
            whole = fluxes[0][end] + jnp.where(row_lane == 0, beside(side_row, 2 * tests + t), 0.0)
            whole = whole + jnp.where(row_lane == columns - 1, beside(side_row, 3 * tests + t), 0.0)
            end_products[end] = end_products[end] + whole * fluxes[1][end]
        east_head = pltpu.roll(head, rows - 1, 0)
        east_weight = pltpu.roll(weight, rows - 1, 0)
        along_rows = along_rows + (east_head - head) * (weight - east_weight)
        old = hb[here, :]
        north_old = jnp.where(at_end, beside(halo, 3 * tests + t), pltpu.roll(old, columns - 1, 1))
        north_weight = jnp.where(at_end, beside(side, tests + t), pltpu.roll(weight, columns - 1, 1))
        along_columns = along_columns + (north_old - old) * (weight - north_weight)
        start_face = start_face + (old[:, :LANES] - beside(halo, 2 * tests + t)) * (
            beside(side, t) - weight[:, :LANES]
        )
    cond_east = pltpu.roll(conduct, rows - 1, 0)
    face = 2.0 * conduct * cond_east / (conduct + cond_east)
    face = jnp.where(row == rows - 1, 0.0, face)
    share = implicit_ratio * face * face * along_rows
    total = share + pltpu.roll(share, 1, 0)
    cond_north = jnp.where(at_end, beside(halo, 5 * tests), pltpu.roll(conduct, columns - 1, 1))
    face = 2.0 * conduct * cond_north / (conduct + cond_north)
    share = explicit_ratio * face * face * along_columns
    cond_start = conduct[:, :LANES]
    cond_south = jnp.broadcast_to(beside(halo, 4 * tests), (rows, LANES))
    face = 2.0 * cond_start * cond_south / (cond_start + cond_south)
    start_share = explicit_ratio * face * face * start_face
    start_share = jnp.concatenate([start_share, jnp.zeros((rows, columns - LANES), jnp.float32)], axis=1)
    total = total + share + jnp.where(at_start, start_share, pltpu.roll(share, 1, 1))
    scale = -1.0 / implicit_ratio
    total = total + jnp.where(row == 0, scale * end_products[0], 0.0)
    total = total + jnp.where(row == rows - 1, scale * end_products[1], 0.0)
    sensitivity[...] = total * (0.5 / conduct)


def in_hbm(x):
    return pltpu.with_memory_space_constraint(x, pltpu.HBM)


def f32(*shape):
    return jax.ShapeDtypeStruct(shape, jnp.float32)


VMEM = pl.BlockSpec(memory_space=pltpu.VMEM)
SIDE_COST = 1000
KEEP_COST = 7000000000
PARAMS = pltpu.CompilerParams(vmem_limit_bytes=40 * 1024 * 1024)


def per_device(head_before, log_conductivity, fixed_mask, well_cells, pump_rates, adjoint_seed):
    tests, rows, columns = head_before.shape
    tiles = columns // LANES
    devices = lax.axis_size("gx")
    peers = lax.axis_size("gy")
    hb = head_before.reshape(tests * rows, columns)
    seed = adjoint_seed.reshape(tests * rows, columns)

    side = f32(rows, LANES)
    part = f32(tiles * tests * rows, LANES)
    out_rows = 2 * tests + 3
    back_rows = 2 * tests + 2

    def exchanged(rows_of_all):
        flat = rows_of_all.reshape(devices, 1, rows_of_all.size // devices)
        return lax.all_to_all(flat, "gx", 0, 0).reshape(rows_of_all.shape)

    anywhere = pl.BlockSpec(memory_space=pl.ANY)
    message, heads_part, adjoint_part, first, last, to_right, to_left, own = pl.pallas_call(
        functools.partial(local_kernel, rows, tests, columns * peers),
        in_specs=[anywhere] * 6,
        out_specs=[anywhere] + [VMEM] * 7,
        out_shape=[f32(devices * out_rows, LANES), part, part] + [f32(rows, columns)] * 2 + [side] * 3,
        scratch_shapes=[pltpu.SMEM((tests,), jnp.int32), pltpu.SMEM((tests,), jnp.float32)]
        + [pltpu.VMEM((tests * rows, columns), jnp.float32)] * 2
        + [pltpu.VMEM((rows, columns), jnp.float32), pltpu.VMEM((rows, columns), jnp.int32)]
        + [pltpu.VMEM((devices * out_rows, LANES), jnp.float32)]
        + [pltpu.SemaphoreType.DMA((6,)), pltpu.SemaphoreType.DMA]
        + [pltpu.VMEM((tiles * tests * rows, LANES), jnp.float32)] * 2
        + [pltpu.VMEM((rows * tiles, LANES), jnp.float32)] * 7,
        compiler_params=PARAMS,
        name="local",
    )(*[in_hbm(x) for x in (well_cells, pump_rates, hb, seed, log_conductivity, fixed_mask)])
    got = exchanged(message)
    from_right = lax.ppermute(to_left, "gy", [(i + 1, i) for i in range(peers - 1)])
    from_left = lax.ppermute(to_right, "gy", [(i, i + 1) for i in range(peers - 1)])
    from_left = pl.pallas_call(
        keep_kernel,
        in_specs=[VMEM],
        out_specs=VMEM,
        out_shape=side,
        compiler_params=PARAMS,
        cost_estimate=pl.CostEstimate(flops=KEEP_COST, bytes_accessed=0, transcendentals=0),
        name="keep",
    )(from_left)
    side_part, side_first, side_last, side_rows = pl.pallas_call(
        functools.partial(side_kernel, rows, tests),
        in_specs=[VMEM] * 3,
        out_specs=[VMEM] * 4,
        out_shape=[side] * 3 + [f32(SUBLANES, LANES)],
        compiler_params=PARAMS,
        cost_estimate=pl.CostEstimate(flops=SIDE_COST, bytes_accessed=0, transcendentals=0),
        name="sides",
    )(from_left, from_right, own)
    reply = pl.pallas_call(
        functools.partial(line_kernel, devices, tests),
        in_specs=[VMEM] * 2,
        out_specs=VMEM,
        out_shape=f32(devices * back_rows, LANES),
        compiler_params=PARAMS,
        name="line",
    )(got, side_rows)
    answer = exchanged(reply)
    heads, sensitivity = pl.pallas_call(
        functools.partial(final_kernel, rows, tests),
        in_specs=[VMEM] * 12,
        out_specs=[VMEM] * 2,
        out_shape=[f32(tests * rows, columns), f32(rows, columns)],
        scratch_shapes=[pltpu.VMEM((devices + SUBLANES, LANES), jnp.float32)],
        compiler_params=PARAMS,
        name="final",
    )(
        hb, log_conductivity, heads_part, adjoint_part, first, last, answer, from_left, from_right,
        side_part, side_first, side_last,
    )
    return heads.reshape(tests, rows, columns), sensitivity


def solution(mesh):
    return jax.shard_map(
        per_device,
        mesh=mesh,
        in_specs=(P(None, "gx", "gy"), P("gx", "gy"), P("gx", "gy"), P(), P(), P(None, "gx", "gy")),
        out_specs=(P(None, "gx", "gy"), P("gx", "gy")),
        check_vma=False,
    )
```
